32 devices in a mesh: ens: 4 (over x, core), grid: 8 (over z, y).
Axes of the slice: x: 2, y: 2, z: 4, core: 2. Of those that a mesh axis runs over, the one named last changes fastest.
Arguments:
- embeddings: bfloat16 [8, 1024, 1024], P('ens', 'grid'), may hold values from -20 to 20
- reference_analysis: float32 [100, 1024], P(None, 'grid'), may hold values from -6 to 6
- attention_matrix: bfloat16 [1024, 3072], replicated, may hold values from -8 to 8
- readout_matrix: bfloat16 [1024, 100], replicated, may hold values from -0.1875 to 0.1875
- adjacent_blocks: int32 [16, 3], P('grid'), may hold values from 0 to 15, as said below
- companion_matrix: int32 [7, 8], replicated, may hold values from 0 to 7, as said below
- continent_indicator: int32 [1024], P('grid'), may hold values 0 or 1
- zonal_strip: int32 [1024], P('grid'), may hold values from 0 to 720
Outputs:
- energy_objective: float32 [], replicated
- embedding_sensitivity: float32 [8, 1024, 1024], P('ens', 'grid')
- grad_value_matrix: float32 [1048576], P(('ens', 'grid'))
- grad_dec: float32 [102400], P(('ens', 'grid'))
The draws below stay inside these ranges and needn't reach their ends.
Inputs may be any that keep to these rules, and one draw needn't show every extreme that they name: `adjacent_blocks`: entry 0 of row b is b; entry 1 lies 1 to 2 blocks before b and entry 2 lies 1 to 2 blocks after b, each clamped into 0 to 15. Each row is a perfect matching of the members: companion_matrix[r, companion_matrix[r, m]] = m and companion_matrix[r, m] != m; every two members are partners in exactly one row.
All inputs are finite; a program needn't handle non-finite values. No bound on the sum of `continent_indicator` on one device may be relied on, other than what follows from the above.
Results may differ from the reference program's by a relative error of at most 0.012.
The reference program's roundings to bfloat16 on the way count: a program that leaves them out, or rounds other values in their place, can miss the bound.
Values may be sent and summed in bfloat16 or wider, within the bound.
A program may use at most 128 MiB of HBM per device.

```python
import math
import jax
import jax.numpy as jnp
from jax import lax

D = 1024
HEADS = 16
CH = 100
QB = 64
R_BLK = 2
NB = 3
SCORED_ENTRIES = 128
NLAT = 721
MEMBERS = 8
ROUNDS = 7
NPTS = 1024
NBLOCKS = 16


def draw_embeddings(key, part):
    array_shape = (MEMBERS, NPTS, D)
    values = jax.random.normal(jax.random.fold_in(key, 1), array_shape, jnp.float32)
    return jnp.clip(values, -20.0, 20.0).astype(jnp.bfloat16)


def draw_attention_matrix(key, part):
    values = jnp.clip(jax.random.normal(jax.random.fold_in(key, 1), (D, 3 * D), jnp.float32), -6.0, 6.0) / math.sqrt(D)
    return jnp.clip(values, -8.0, 8.0).astype(jnp.bfloat16)


def draw_adjacent_blocks(key, part):
    blocks = jnp.arange(NBLOCKS, dtype=jnp.int32)
    back_steps = jax.random.randint(jax.random.fold_in(key, 1), (NBLOCKS,), 1, R_BLK + 1, dtype=jnp.int32)
    ahead_steps = jax.random.randint(jax.random.fold_in(key, 2), (NBLOCKS,), 1, R_BLK + 1, dtype=jnp.int32)
    before = jnp.clip(blocks - back_steps, 0, NBLOCKS - 1)
    after = jnp.clip(blocks + ahead_steps, 0, NBLOCKS - 1)
    return jnp.stack([blocks, before, after], axis=1).astype(jnp.int32)


def draw_companion_matrix(key, part):
    relabel = jax.random.permutation(jax.random.fold_in(key, 1), MEMBERS).astype(jnp.int32)
    order = jax.random.permutation(jax.random.fold_in(key, 2), ROUNDS).astype(jnp.int32)
    inverse = jnp.argsort(relabel, stable=True).astype(jnp.int32)
    seats = inverse[None, :]
    round_ids = order[:, None]
    last_seat = MEMBERS - 1
    facing = jnp.mod(2 * round_ids - seats, last_seat)
    partner_seat = jnp.where(seats == last_seat, round_ids, jnp.where(seats == round_ids, last_seat, facing))
    return relabel[partner_seat].astype(jnp.int32)


def set_ends(entries, own_key, least, largest):
    index_at = [jax.random.randint(jax.random.fold_in(own_key, axis), (), 0, length) for axis, length in enumerate(entries.shape)]
    longest = entries.shape.index(max(entries.shape))
    next_to = index_at[:longest] + [(index_at[longest] + 1) % entries.shape[longest]] + index_at[longest + 1:]
    return entries.at[tuple(index_at)].set(least).at[tuple(next_to)].set(largest)


def steps_of(key, shape, shards, smallest, largest):
    def one(position, blocks):
        heights = jax.random.uniform(jax.random.fold_in(jax.random.fold_in(key, 6), position), (blocks,), jnp.float32, smallest / len(shards), largest / len(shards))
        return jnp.repeat(jnp.exp(heights), shape[position] // blocks).reshape((-1,) + (1,) * (len(shape) - position - 1))

    factor_of = one(*shards[0])
    for cut in shards[1:]:
        factor_of = factor_of * one(*cut)
    return factor_of


def gaussian(stream_key, extent, spread, reach, cuts=(), kind=jnp.bfloat16):
    result = jax.random.normal(stream_key, extent, jnp.float32) * spread
    if len(cuts) > 0:
        result = steps_of(stream_key, extent, cuts, -0.22, 0.18) * result
    return jnp.clip(result, min=-reach, max=reach).astype(kind)


def setup_inputs(seed: int = 0) -> dict:
    streams_of = jax.random.split(jax.random.key(seed), 9)
    embeddings = draw_embeddings(jax.random.fold_in(streams_of[8], 71), 0)
    reference_analysis = gaussian(streams_of[1], (CH, NPTS), 1.0, 6.0, ((1, 8),), jnp.float32)
    attention_matrix = draw_attention_matrix(jax.random.fold_in(streams_of[8], 71), 0)
    readout_matrix = gaussian(streams_of[3], (D, CH), D ** -0.5, 0.1875)
    adjacent_blocks = draw_adjacent_blocks(jax.random.fold_in(streams_of[8], 71), 0)
    companion_matrix = draw_companion_matrix(jax.random.fold_in(streams_of[8], 71), 0)
    continent_indicator = set_ends((jax.random.randint(streams_of[6], (NPTS,), 0, 10) < 3).astype(jnp.int32), jax.random.fold_in(streams_of[6], 1), 0, 1)
    zonal_strip = set_ends(jax.random.randint(streams_of[7], (NPTS,), 0, NLAT), jax.random.fold_in(streams_of[7], 1), 0, NLAT - 1).astype(jnp.int32)
    return dict(embeddings=embeddings, reference_analysis=reference_analysis, attention_matrix=attention_matrix, readout_matrix=readout_matrix, adjacent_blocks=adjacent_blocks, companion_matrix=companion_matrix, continent_indicator=continent_indicator, zonal_strip=zonal_strip)


EPSILON = 1e-06

def rms_scale(values):
    return lax.rsqrt(lax.optimization_barrier(jnp.mean(values * values, axis=-1, keepdims=True)) + EPSILON)

def sample_evaluate(embedded_grid, attention_matrix, readout_matrix, adjacent_blocks):
    block_count = embedded_grid.shape[0] // QB
    model_width = embedded_grid.shape[1]
    head_dim = model_width // HEADS
    score_scale = 1.0 / math.sqrt(head_dim)
    lat_float = embedded_grid.astype(jnp.float32)
    inv_first = rms_scale(lat_float)
    normed = (lat_float * inv_first).astype(jnp.bfloat16)
    projected = jnp.dot(normed, attention_matrix, preferred_element_type=jnp.float32).astype(jnp.bfloat16)
    queries = projected[:, :model_width].reshape(block_count, QB, HEADS, head_dim)
    keyval = projected[:, model_width:].reshape(block_count, QB, 2 * model_width)
    picked = keyval[adjacent_blocks.reshape(-1)].reshape(block_count, NB * QB, 2, HEADS, head_dim)
    window_keys = picked[:, :, 0]
    window_values = picked[:, :, 1]
    scores = jnp.einsum('bqhe,bkhe->bhqk', queries.astype(jnp.float32), window_keys.astype(jnp.float32)) * score_scale
    highest = lax.optimization_barrier(jnp.max(scores, axis=-1, keepdims=True))
    exp_scores = jnp.exp(scores - highest)
    attention = exp_scores / lax.optimization_barrier(jnp.sum(exp_scores, axis=-1, keepdims=True))
    attention16 = attention.astype(jnp.bfloat16)
    attended = jnp.einsum('bhqk,bkhe->bqhe', attention16.astype(jnp.float32), window_values.astype(jnp.float32))
    residual_state = lat_float + attended.reshape(embedded_grid.shape[0], model_width)
    inv_second = rms_scale(residual_state)
    internal_activation = (residual_state * inv_second).astype(jnp.bfloat16)
    predicted_grid = lax.dot_general(readout_matrix, internal_activation, (((0,), (1,)), ((), ())), preferred_element_type=jnp.float32)
    retained_entries = (lat_float, inv_first, normed, queries, window_keys, window_values, attention, attention16, residual_state, inv_second, internal_activation)
    return (predicted_grid, retained_entries)

def objective_factors(predicted_grids, reference_analysis, companion_matrix, continent_indicator, zonal_strip):
    sample_count, variable_indices, location_count = predicted_grids.shape
    region_count = location_count // SCORED_ENTRIES
    phase = (zonal_strip.astype(jnp.float32) + 0.5) * (math.pi / NLAT) - 0.5 * math.pi
    location_factors = (jnp.cos(phase) * (1.0 + continent_indicator.astype(jnp.float32))).reshape(region_count, SCORED_ENTRIES)
    region_sequence = predicted_grids.reshape(sample_count, variable_indices, region_count, SCORED_ENTRIES)
    target_patches = reference_analysis.reshape(variable_indices, region_count, SCORED_ENTRIES)
    error_component = region_sequence - target_patches[None]
    observed_separation = jnp.sqrt(lax.optimization_barrier(jnp.sum(location_factors * error_component * error_component, axis=-1)) + EPSILON)
    round_of = (jnp.arange(variable_indices, dtype=jnp.int32)[:, None] + jnp.arange(region_count, dtype=jnp.int32)[None, :]) % ROUNDS
    partner = jnp.transpose(companion_matrix[round_of], (2, 0, 1))
    partner_pick = (partner[..., None] == jnp.arange(sample_count, dtype=jnp.int32)).astype(jnp.float32)
    partner_patches = jnp.einsum('mcjn,ncjp->mcjp', partner_pick, region_sequence, precision=lax.Precision.HIGHEST)
    dispersion_component = region_sequence - partner_patches
    mutual_separation = jnp.sqrt(lax.optimization_barrier(jnp.sum(location_factors * dispersion_component * dispersion_component, axis=-1)) + EPSILON)
    total = jnp.sum(observed_separation) - 0.5 * jnp.sum(mutual_separation)
    energy_objective = total / (sample_count * variable_indices * region_count)
    predicted_sensitivity = location_factors * error_component / observed_separation[..., None] - location_factors * dispersion_component / mutual_separation[..., None]
    return (energy_objective, predicted_sensitivity.reshape(sample_count, variable_indices, location_count))

def sample_reverse(embedded_grid, predicted_sensitivity, attention_matrix, readout_matrix, adjacent_blocks):
    predicted_grid, retained_entries = sample_evaluate(embedded_grid, attention_matrix, readout_matrix, adjacent_blocks)
    lat_float, inv_first, normed, queries, window_keys, window_values, attention, attention16, residual_state, inv_second, internal_activation = retained_entries
    location_count, model_width = embedded_grid.shape
    block_count = location_count // QB
    head_dim = model_width // HEADS
    score_scale = 1.0 / math.sqrt(head_dim)
    sensitivity_reduced16 = predicted_sensitivity.astype(jnp.bfloat16)
    grad_dec = lax.dot_general(internal_activation, sensitivity_reduced16, (((0,), (1,)), ((), ())), preferred_element_type=jnp.float32)
    grad_hidden = lax.dot_general(sensitivity_reduced16, readout_matrix, (((0,), (1,)), ((), ())), preferred_element_type=jnp.float32)
    unit_state = residual_state * inv_second
    grad_state = inv_second * (grad_hidden - unit_state * lax.optimization_barrier(jnp.mean(grad_hidden * unit_state, axis=-1, keepdims=True)))
    grad_out16 = grad_state.astype(jnp.bfloat16).reshape(block_count, QB, HEADS, head_dim).astype(jnp.float32)
    grad_attention = jnp.einsum('bqhe,bkhe->bhqk', grad_out16, window_values.astype(jnp.float32))
    grad_values = jnp.einsum('bhqk,bqhe->bkhe', attention16.astype(jnp.float32), grad_out16)
    grad_scores = (attention * (grad_attention - lax.optimization_barrier(jnp.sum(attention * grad_attention, axis=-1, keepdims=True))) * score_scale).astype(jnp.bfloat16)
    grad_queries = jnp.einsum('bhqk,bkhe->bqhe', grad_scores.astype(jnp.float32), window_keys.astype(jnp.float32))
    grad_keys = jnp.einsum('bhqk,bqhe->bkhe', grad_scores.astype(jnp.float32), queries.astype(jnp.float32))
    grad_window = jnp.stack([grad_keys, grad_values], axis=2).reshape(block_count * NB, QB, 2 * model_width)
    gathered_back = jax.ops.segment_sum(grad_window, adjacent_blocks.reshape(-1), num_segments=block_count)
    grad_proj = jnp.concatenate([grad_queries.reshape(location_count, model_width), gathered_back.reshape(location_count, 2 * model_width)], axis=-1).astype(jnp.bfloat16)
    grad_value_matrix = lax.dot_general(normed, grad_proj[:, 2 * model_width:], (((0,), (0,)), ((), ())), preferred_element_type=jnp.float32)
    grad_normed = lax.dot_general(grad_proj, attention_matrix, (((1,), (1,)), ((), ())), preferred_element_type=jnp.float32)
    unit_input = lat_float * inv_first
    grad_latent = grad_state + inv_first * (grad_normed - unit_input * lax.optimization_barrier(jnp.mean(grad_normed * unit_input, axis=-1, keepdims=True)))
    return (grad_latent, grad_value_matrix, grad_dec)

def reference(embeddings, reference_analysis, attention_matrix, readout_matrix, adjacent_blocks, companion_matrix, continent_indicator, zonal_strip):

    def evaluation_only(embedded_grid):
        return sample_evaluate(embedded_grid, attention_matrix, readout_matrix, adjacent_blocks)[0]
    predicted_grids = lax.map(evaluation_only, embeddings)
    energy_objective, predicted_sensitivity = objective_factors(predicted_grids, reference_analysis, companion_matrix, continent_indicator, zonal_strip)

    def reverse_only(inputs):
        return sample_reverse(inputs[0], inputs[1], attention_matrix, readout_matrix, adjacent_blocks)
    embedding_sensitivity, value_factors, readout_factors = lax.map(reverse_only, (embeddings, predicted_sensitivity))
    return (energy_objective, embedding_sensitivity, lax.optimization_barrier(jnp.sum(value_factors, axis=0)).reshape(-1), lax.optimization_barrier(jnp.sum(readout_factors, axis=0)).reshape(-1))
```

```python
import functools
import math

import jax
import jax.numpy as jnp
from jax import lax
from jax.experimental import pallas as pl
from jax.experimental.pallas import tpu as pltpu
from jax.sharding import PartitionSpec as P

HEADS = 16
QB = 64
R_BLK = 2
NB = 3
SCORED_ENTRIES = 128
NLAT = 721
EPSILON = 1e-06
RIM = R_BLK * QB
LANES = 128
NEG = -1e30

F32 = jnp.float32
BF16 = jnp.bfloat16
MESH = pl.DeviceIdType.MESH


def mm(a, b):
    return lax.dot_general(a, b, (((1,), (0,)), ((), ())), preferred_element_type=F32)


def mm_nt(a, b):
    return lax.dot_general(a, b, (((1,), (1,)), ((), ())), preferred_element_type=F32)


def mm_tn(a, b):
    return lax.dot_general(a, b, (((0,), (0,)), ((), ())), preferred_element_type=F32)


def rms_scale(values):
    return lax.rsqrt(jnp.mean(values * values, axis=-1, keepdims=True) + EPSILON)


def kernel(
    n_ens, n_grid, channels,
    adj_ref, comp_ref, x_ref, ref_ref, w_ref, r_ref, weight_ref,
    tot_ref, out_ref, gv_ref, gd_ref,
    nrm, q_s, kv, cnt_s, ac_s, state, hid, go, gq, gkv, fc,
    vp, rc0, s1, rc1, s2, r2, gnr, gnx, tq, tg,
    halo_send, halo_recv, fc_send, fc_recv, core_send, core_recv,
    x_send, x_recv, g_send, g_recv, back_send, back_recv,
    tq_send, tq_recv, tg_send, tg_recv,
):
    members, points, width = x_ref.shape
    ext = points + 2 * RIM
    nblk = points // QB
    pairs = width // LANES
    rounds = comp_ref.shape[0]
    patches = points // SCORED_ENTRIES
    rows_pp = width // (n_ens * n_grid)
    fold = max(1, 16 // rows_pp)
    wide = width // fold
    n_far = n_ens // 2
    e = lax.axis_index("ens")
    g = lax.axis_index("grid")
    core = e % 2
    far = e // 2
    scale = 1.0 / math.sqrt(width // HEADS)

    def ens_copy(src, dst, ss, rs, to):
        return pltpu.make_async_remote_copy(
            src_ref=src, dst_ref=dst, send_sem=ss, recv_sem=rs,
            device_id={"ens": to}, device_id_type=MESH,
        )

    def grid_copy(src, dst, ss, rs, to):
        return pltpu.make_async_remote_copy(
            src_ref=src, dst_ref=dst, send_sem=ss, recv_sem=rs,
            device_id={"grid": to}, device_id_type=MESH,
        )

    for m in range(members):
        lat = x_ref[m].astype(F32)
        nrm[m, RIM : RIM + points] = (lat * rms_scale(lat)).astype(BF16)

    @pl.when(g == 0)
    def _():
        nrm[:, :RIM] = jnp.zeros((members, RIM, width), BF16)

    @pl.when(g == n_grid - 1)
    def _():
        nrm[:, RIM + points :] = jnp.zeros((members, RIM, width), BF16)

    barrier = pltpu.get_barrier_semaphore()
    for k in range(1, n_ens):
        pl.semaphore_signal(barrier, inc=1, device_id={"ens": (e + k) % n_ens}, device_id_type=MESH)
    for k in range(1, n_grid):
        pl.semaphore_signal(barrier, inc=1, device_id={"grid": (g + k) % n_grid}, device_id_type=MESH)
    pl.semaphore_wait(barrier, n_ens + n_grid - 2)

    up = grid_copy(nrm.at[:, pl.ds(points, RIM)], nrm.at[:, pl.ds(0, RIM)],
                   halo_send.at[0], halo_recv.at[0], (g + 1) % n_grid)
    down = grid_copy(nrm.at[:, pl.ds(RIM, RIM)], nrm.at[:, pl.ds(RIM + points, RIM)],
                     halo_send.at[1], halo_recv.at[1], (g + n_grid - 1) % n_grid)

    @pl.when(g < n_grid - 1)
    def _():
        up.start()

    @pl.when(g > 0)
    def _():
        down.start()

    tile = 512

    @pl.loop(0, width // tile)
    def _(t):
        own = nrm[:, RIM : RIM + points].reshape(members * points, width)
        c = pl.multiple_of(t * tile, tile)
        q_s[:, :, pl.ds(c, tile)] = mm(own, w_ref[:, pl.ds(c, tile)]).astype(BF16).reshape(
            members, points, tile
        )

    @pl.loop(0, 2 * width // tile)
    def _(t):
        own = nrm[:, RIM : RIM + points].reshape(members * points, width)
        c = pl.multiple_of(t * tile, tile)
        wt = w_ref[:, pl.ds(pl.multiple_of(c + width, tile), tile)]
        kv[:, RIM : RIM + points, pl.ds(c, tile)] = mm(own, wt).astype(BF16).reshape(
            members, points, tile
        )

    col = lax.broadcasted_iota(jnp.int32, (1, ext), 1)
    for b in range(nblk):
        count = jnp.zeros((1, ext), F32)
        for n in range(NB):
            first = (adj_ref[b, n] - g * nblk + R_BLK) * QB
            count += jnp.where((col >= first) & (col < first + QB), 1.0, 0.0)
        rows = jnp.broadcast_to(count, (QB, ext))
        cnt_s[b * QB : (b + 1) * QB] = rows
        cnt_s[points + b * QB : points + (b + 1) * QB] = rows

    @pl.when(g > 0)
    def _():
        up.wait_recv()

    @pl.when(g < n_grid - 1)
    def _():
        down.wait_recv()

    @pl.loop(0, 2 * width // tile)
    def _(t):
        c = pl.multiple_of(t * tile, tile)
        wt = w_ref[:, pl.ds(pl.multiple_of(c + width, tile), tile)]
        rim = jnp.concatenate(
            [nrm[:, :RIM].reshape(members * RIM, width),
             nrm[:, RIM + points :].reshape(members * RIM, width)], axis=0
        )
        res = mm(rim, wt).astype(BF16)
        kv[:, :RIM, pl.ds(c, tile)] = res[: members * RIM].reshape(members, RIM, tile)
        kv[:, RIM + points :, pl.ds(c, tile)] = res[members * RIM :].reshape(members, RIM, tile)

    head_a = lax.broadcasted_iota(jnp.int32, (points, LANES), 1) < LANES // 2

    def stacked(v):
        zero = jnp.zeros_like(v)
        return jnp.concatenate([jnp.where(head_a, v, zero), jnp.where(head_a, zero, v)], axis=0)

    def merged(v):
        return jnp.where(head_a, v[:points], v[points:])

    def place(it):
        m = it // pairs
        c = pl.multiple_of((it % pairs) * LANES, LANES)
        return m, pl.ds(c, LANES), pl.ds(pl.multiple_of(c + width, LANES), LANES)

    @pl.loop(0, members * pairs)
    def _(it):
        m, ck, cv = place(it)
        s = mm_nt(stacked(q_s[m, :, ck]), kv[m, :, ck]) * scale
        cnt = cnt_s[...]
        s = jnp.where(cnt > 0.0, s, NEG)
        ex = jnp.exp(s - jnp.max(s, axis=-1, keepdims=True)) * cnt
        a = ex * (1.0 / jnp.sum(ex, axis=-1, keepdims=True))
        ac_s[it] = a
        state[m, :, ck] = merged(mm(a.astype(BF16), kv[m, :, cv]))

    for m in range(members):
        st = x_ref[m].astype(F32) + state[m]
        state[m] = st
        h = (st * rms_scale(st)).astype(BF16)
        hid[m * points : (m + 1) * points] = h
        fc[e, m] = mm(h, r_ref[...])

    fcs = []
    for k in range(1, n_ens):
        cp = ens_copy(fc.at[e], fc.at[e], fc_send.at[k], fc_recv.at[k], (e + k) % n_ens)
        cp.start()
        fcs.append(cp)
    for cp in fcs:
        cp.wait()

    lane = lax.broadcasted_iota(jnp.int32, (1, LANES), 1)
    valid = lane < channels
    total = jnp.zeros((1, LANES), F32)
    g16 = []
    for m in range(members):
        parts = []
        for j in range(patches):
            rows = slice(j * SCORED_ENTRIES, (j + 1) * SCORED_ENTRIES)
            rnd = (lane + g * patches + j) % rounds
            partner = jnp.zeros((1, LANES), jnp.int32)
            for r in range(rounds):
                partner = jnp.where(rnd == r, comp_ref[r, e * members + m], partner)
            f = fc[e, m, rows]
            pf = jnp.zeros_like(f)
            for n in range(n_ens * members):
                pf = jnp.where(partner == n, fc[n // members, n % members, rows], pf)
            wgt = weight_ref[rows]
            err = f - ref_ref[rows]
            dif = f - pf
            dt = jnp.sqrt(jnp.sum(wgt * err * err, axis=0, keepdims=True) + EPSILON)
            dp = jnp.sqrt(jnp.sum(wgt * dif * dif, axis=0, keepdims=True) + EPSILON)
            total += jnp.where(valid, dt - 0.5 * dp, 0.0)
            parts.append((wgt * err / dt - wgt * dif / dp).astype(BF16))
        g16.append(jnp.concatenate(parts, axis=0) if patches > 1 else parts[0])
    g_all = jnp.concatenate(g16, axis=0)

    tq[e] = jnp.broadcast_to(jnp.sum(total, axis=-1, keepdims=True), (8, LANES))
    tqs = []
    for k in range(1, n_ens):
        cp = ens_copy(tq.at[e], tq.at[e], tq_send.at[k], tq_recv.at[k], (e + k) % n_ens)
        cp.start()
        tqs.append(cp)

    for m in range(members):
        gh = mm_nt(g16[m], r_ref[...])
        st = state[m]
        inv = rms_scale(st)
        y = st * inv
        gs = inv * (gh - y * jnp.mean(gh * y, axis=-1, keepdims=True))
        out_ref[m] = gs
        go[m] = gs.astype(BF16)

    @pl.loop(0, members * pairs)
    def _(it):
        m, ck, cv = place(it)
        gkv[m, :, cv] = mm_tn(ac_s[it].astype(BF16), stacked(go[m, :, ck])).astype(BF16)

    per_ens = width // n_ens

    def folded(v, cols):
        v = v.reshape(n_grid, rows_pp, cols)
        if fold > 1:
            step = cols // fold
            v = jnp.concatenate([v[:, :, i * step : (i + 1) * step] for i in range(fold)], axis=1)
        return v.astype(BF16)

    @pl.loop(0, n_ens)
    def _(qd):
        d = pl.ds(pl.multiple_of(qd * per_ens, per_ens), per_ens)
        acc = jnp.zeros((per_ens, width), F32)
        for m in range(members):
            acc += mm_tn(nrm[m, :, d], gkv[m, :, width:])
        vp[qd, :, :, :wide] = folded(acc, width)
        dec = mm_tn(hid[:, d], g_all)
        if fold > 1:
            dec = jnp.concatenate(
                [dec, jnp.zeros((per_ens, LANES * (fold - 1)), F32)], axis=1
            )
        vp[qd, :, :, wide:] = folded(dec, LANES * fold)

    cores = []
    for k in range(n_far):
        f = (far + 1 + k) % n_far
        cp = ens_copy(vp.at[2 * f + 1 - core], rc0.at[f], core_send.at[k], core_recv.at[k],
                      2 * far + 1 - core)
        cp.start()
        cores.append(cp)

    for cp in tqs:
        cp.wait()
    tg[g] = functools.reduce(lambda a, b: a + b, [tq[i] for i in range(n_ens)])
    tgs = []
    for k in range(1, n_grid):
        cp = grid_copy(tg.at[g], tg.at[g], tg_send.at[k], tg_recv.at[k], (g + k) % n_grid)
        cp.start()
        tgs.append(cp)

    def back(it):
        m, ck, cv = place(it)
        a = ac_s[it]
        da = mm_nt(stacked(go[m, :, ck]), kv[m, :, cv])
        ds = a * (da - jnp.sum(a * da, axis=-1, keepdims=True)) * scale
        ds = ds.astype(BF16)
        gq[m, :, ck] = merged(mm(ds, kv[m, :, ck])).astype(BF16)
        gkv[m, :, ck] = mm_tn(ds, stacked(q_s[m, :, ck])).astype(BF16)

    split = 2

    @pl.loop(0, split)
    def _(it):
        back(it)

    xs = []
    for k in range(n_far - 1):
        cores[k].wait()
        f = (far + 1 + k) % n_far
        s1[k] = (vp[2 * f + core].astype(F32) + rc0[f].astype(F32)).astype(BF16)
        cp = ens_copy(s1.at[k], rc1.at[k], x_send.at[k], x_recv.at[k], 2 * f + core)
        cp.start()
        xs.append(cp)
    cores[n_far - 1].wait()

    @pl.loop(split, members * pairs)
    def _(it):
        back(it)

    dt_tile = 256

    @pl.loop(0, width // dt_tile)
    def _(t):
        d = pl.ds(pl.multiple_of(t * dt_tile, dt_tile), dt_tile)
        rim = jnp.concatenate(
            [gkv[:, :RIM].reshape(members * RIM, 2 * width),
             gkv[:, RIM + points :].reshape(members * RIM, 2 * width)], axis=0
        )
        res = mm_nt(rim, w_ref[d, width:]).astype(BF16)
        gnr[:, :, :, d] = res.reshape(2, members, RIM, dt_tile)

    to_prev = grid_copy(gnr.at[0], gnx.at[0], back_send.at[0], back_recv.at[0],
                        (g + n_grid - 1) % n_grid)
    to_next = grid_copy(gnr.at[1], gnx.at[1], back_send.at[1], back_recv.at[1], (g + 1) % n_grid)

    @pl.when(g > 0)
    def _():
        to_prev.start()

    @pl.when(g < n_grid - 1)
    def _():
        to_next.start()

    for cp in xs:
        cp.wait()
    part = vp[2 * far + core].astype(F32) + rc0[far].astype(F32)
    for k in range(n_far - 1):
        part += rc1[k].astype(F32)
    s2[...] = part.astype(BF16)
    gcs = []
    for k in range(1, n_grid):
        to = (g + k) % n_grid
        cp = grid_copy(s2.at[to], r2.at[k], g_send.at[k], g_recv.at[k], to)
        cp.start()
        gcs.append(cp)

    @pl.loop(0, width // dt_tile)
    def _(t):
        d = pl.ds(pl.multiple_of(t * dt_tile, dt_tile), dt_tile)
        res = mm_nt(gq[...].reshape(members * points, width), w_ref[d, :width])
        res += mm_nt(gkv[:, RIM : RIM + points].reshape(members * points, 2 * width),
                     w_ref[d, width:])
        state[:, :, d] = res.reshape(members, points, dt_tile)

    @pl.when(g < n_grid - 1)
    def _():
        to_prev.wait_recv()
        state[:, points - RIM :] += gnx[0].astype(F32)

    @pl.when(g > 0)
    def _():
        to_next.wait_recv()
        state[:, :RIM] += gnx[1].astype(F32)

    for m in range(members):
        lat = x_ref[m].astype(F32)
        inv = rms_scale(lat)
        y = lat * inv
        gn = state[m]
        out_ref[m] += inv * (gn - y * jnp.mean(gn * y, axis=-1, keepdims=True))

    for cp in tgs:
        cp.wait()
    tot_ref[...] = functools.reduce(lambda a, b: a + b, [tg[i] for i in range(n_grid)])

    for cp in gcs:
        cp.wait()
    acc = s2[g].astype(F32)
    for k in range(1, n_grid):
        acc += r2[k].astype(F32)
    for i in range(fold):
        gv_ref[:, i * wide : (i + 1) * wide] = acc[i * rows_pp : (i + 1) * rows_pp, :wide]
    gd_ref[...] = acc[:rows_pp, wide:]

    @pl.when(g < n_grid - 1)
    def _():
        up.wait_send()
        to_next.wait_send()

    @pl.when(g > 0)
    def _():
        down.wait_send()
        to_prev.wait_send()


def per_device(
    embeddings,
    reference_analysis,
    attention_matrix,
    readout_matrix,
    adjacent_blocks,
    companion_matrix,
    continent_indicator,
    zonal_strip,
):
    members, points, width = embeddings.shape
    channels = reference_analysis.shape[0]
    n_ens, n_grid = lax.axis_size("ens"), lax.axis_size("grid")
    ext = points + 2 * RIM
    pairs = width // LANES
    rows_pp = width // (n_ens * n_grid)
    fold = max(1, 16 // rows_pp)
    chunk = (rows_pp * fold, width // fold + LANES)
    n_far = n_ens // 2
    phase = (zonal_strip.astype(F32) + 0.5) * (math.pi / NLAT) - 0.5 * math.pi
    weight = (jnp.cos(phase) * (1.0 + continent_indicator.astype(F32)))[:, None]
    target = jnp.pad(reference_analysis.T, ((0, 0), (0, LANES - channels)))
    readout = jnp.pad(readout_matrix, ((0, 0), (0, LANES - channels)))
    vmem = pl.BlockSpec(memory_space=pltpu.VMEM)
    smem = pl.BlockSpec(memory_space=pltpu.SMEM)
    dma = pltpu.SemaphoreType.DMA
    V = pltpu.VMEM
    scratch = [
        V((members, ext, width), BF16),
        V((members, points, width), BF16),
        V((members, ext, 2 * width), BF16),
        V((2 * points, ext), F32),
        V((members * pairs, 2 * points, ext), F32),
        V((members, points, width), F32),
        V((members * points, width), BF16),
        V((members, points, width), BF16),
        V((members, points, width), BF16),
        V((members, ext, 2 * width), BF16),
        V((n_ens, members, points, LANES), F32),
        V((n_ens, n_grid) + chunk, BF16),
        V((n_far, n_grid) + chunk, BF16),
        V((max(1, n_far - 1), n_grid) + chunk, BF16),
        V((max(1, n_far - 1), n_grid) + chunk, BF16),
        V((n_grid,) + chunk, BF16),
        V((n_grid,) + chunk, BF16),
        V((2, members, RIM, width), BF16),
        V((2, members, RIM, width), BF16),
        V((n_ens, 8, LANES), F32),
        V((n_grid, 8, LANES), F32),
        dma((2,)), dma((2,)),
        dma((n_ens,)), dma((n_ens,)),
        dma((n_far,)), dma((n_far,)),
        dma((n_far,)), dma((n_far,)),
        dma((n_grid,)), dma((n_grid,)),
        dma((2,)), dma((2,)),
        dma((n_ens,)), dma((n_ens,)),
        dma((n_grid,)), dma((n_grid,)),
    ]
    total, sens, grad_value, grad_dec = pl.pallas_call(
        functools.partial(kernel, n_ens, n_grid, channels),
        out_shape=(
            jax.ShapeDtypeStruct((8, LANES), F32),
            jax.ShapeDtypeStruct((members, points, width), F32),
            jax.ShapeDtypeStruct((rows_pp, width), F32),
            jax.ShapeDtypeStruct((rows_pp, LANES), F32),
        ),
        in_specs=[smem, smem] + [vmem] * 5,
        out_specs=(vmem,) * 4,
        scratch_shapes=scratch,
        compiler_params=pltpu.CompilerParams(
            collective_id=0, has_side_effects=True, vmem_limit_bytes=60 * 1024 * 1024
        ),
    )(adjacent_blocks, companion_matrix, embeddings, target, attention_matrix, readout, weight)
    count = n_ens * members * channels * (points // SCORED_ENTRIES) * n_grid
    return (
        total[0, 0] / count,
        sens,
        grad_value.reshape(-1),
        grad_dec[:, :channels].reshape(-1),
    )


def solution(mesh):
    in_specs = (
        P("ens", "grid", None),
        P(None, "grid"),
        P(),
        P(),
        P("grid", None),
        P(),
        P("grid"),
        P("grid"),
    )
    out_specs = (P(), P("ens", "grid", None), P(("ens", "grid")), P(("ens", "grid")))
    return jax.shard_map(
        per_device, mesh=mesh, in_specs=in_specs, out_specs=out_specs, check_vma=False
    )
```

```python
import functools
import math

import jax
import jax.numpy as jnp
from jax import lax
from jax.experimental import pallas as pl
from jax.experimental.pallas import tpu as pltpu
from jax.sharding import PartitionSpec as P

HEADS = 16
QB = 64
R_BLK = 2
NB = 3
SCORED_ENTRIES = 128
NLAT = 721
EPSILON = 1e-06
RIM = R_BLK * QB
LANES = 128
NEG = -1e30

F32 = jnp.float32
BF16 = jnp.bfloat16
MESH = pl.DeviceIdType.MESH


def mm(a, b):
    return lax.dot_general(a, b, (((1,), (0,)), ((), ())), preferred_element_type=F32)


def mm_nt(a, b):
    return lax.dot_general(a, b, (((1,), (1,)), ((), ())), preferred_element_type=F32)


def mm_tn(a, b):
    return lax.dot_general(a, b, (((0,), (0,)), ((), ())), preferred_element_type=F32)


def rms_scale(values):
    return lax.rsqrt(jnp.mean(values * values, axis=-1, keepdims=True) + EPSILON)


def kernel(
    n_ens, n_grid, channels,
    adj_ref, comp_ref, x_ref, ref_ref, w_hbm, r_ref, land_ref, strip_ref,
    tot_ref, out_ref, gv_ref, gd_ref,
    w_ref, rt, tgt, wgts, nrm, nrm_t, q_s, kv, cnt_s, ac_s, ac_t, state, hid, hid_t, go, gq, gkv, fc,
    vp, rc0, s1, rc1, s2, r2, gnr, gnx, tq, tg,
    w_sem, halo_send, halo_recv, fc_send, fc_recv, core_send, core_recv,
    x_send, x_recv, g_send, g_recv, back_send, back_recv,
    tq_send, tq_recv, tg_send, tg_recv,
):
    members, points, width = x_ref.shape
    ext = points + 2 * RIM
    nblk = points // QB
    pairs = width // LANES
    rounds = comp_ref.shape[0]
    patches = points // SCORED_ENTRIES
    rows_pp = width // (n_ens * n_grid)
    fold = max(1, 16 // rows_pp)
    wide = width // fold
    n_far = n_ens // 2
    pieces = 2 if n_grid % 2 == 0 else 1
    per_piece = n_grid // pieces
    e = lax.axis_index("ens")
    g = lax.axis_index("grid")
    core = e % 2
    far = e // 2
    scale = 1.0 / math.sqrt(width // HEADS)

    def ens_copy(src, dst, ss, rs, to):
        return pltpu.make_async_remote_copy(
            src_ref=src, dst_ref=dst, send_sem=ss, recv_sem=rs,
            device_id={"ens": to}, device_id_type=MESH,
        )

    def grid_copy(src, dst, ss, rs, to):
        return pltpu.make_async_remote_copy(
            src_ref=src, dst_ref=dst, send_sem=ss, recv_sem=rs,
            device_id={"grid": to}, device_id_type=MESH,
        )

    w_copy = pltpu.make_async_copy(w_hbm, w_ref, w_sem)
    w_copy.start()
    barrier = pltpu.get_barrier_semaphore()
    for k in range(1, n_ens):
        pl.semaphore_signal(barrier, inc=1, device_id={"ens": (e + k) % n_ens}, device_id_type=MESH)
    for k in range(1, n_grid):
        pl.semaphore_signal(barrier, inc=1, device_id={"grid": (g + k) % n_grid}, device_id_type=MESH)

    @pl.when(g == 0)
    def _():
        nrm[:, :RIM] = jnp.zeros((members, RIM, width), BF16)

    @pl.when(g == n_grid - 1)
    def _():
        nrm[:, RIM + points :] = jnp.zeros((members, RIM, width), BF16)

    ups, downs = [], []
    for m in range(members):
        lat = x_ref[m].astype(F32)
        nrm[m, RIM : RIM + points] = (lat * rms_scale(lat)).astype(BF16)
        if m == 0:
            pl.semaphore_wait(barrier, n_ens + n_grid - 2)
        up = grid_copy(nrm.at[m, pl.ds(points, RIM)], nrm.at[m, pl.ds(0, RIM)],
                       halo_send.at[m], halo_recv.at[m], (g + 1) % n_grid)
        down = grid_copy(nrm.at[m, pl.ds(RIM, RIM)], nrm.at[m, pl.ds(RIM + points, RIM)],
                         halo_send.at[members + m], halo_recv.at[members + m],
                         (g + n_grid - 1) % n_grid)
        pl.when(g < n_grid - 1)(up.start)
        pl.when(g > 0)(down.start)
        ups.append(up)
        downs.append(down)

    out_ref[...] = jnp.zeros(out_ref.shape, F32)
    out_ref[0, :channels] = r_ref[...].astype(F32)
    out_ref[1, :channels, :points] = ref_ref[...]
    rt[...] = out_ref[0, :LANES].astype(BF16)
    for j in range(patches):
        rows = slice(j * SCORED_ENTRIES, (j + 1) * SCORED_ENTRIES)
        tgt[rows] = out_ref[1, :LANES, rows].T
        phase = (strip_ref[j : j + 1].astype(F32) + 0.5) * (math.pi / NLAT) - 0.5 * math.pi
        wrow = jnp.cos(phase) * (1.0 + land_ref[j : j + 1].astype(F32))
        wgts[rows] = jnp.broadcast_to(wrow, (LANES, SCORED_ENTRIES)).T

    col = lax.broadcasted_iota(jnp.int32, (1, ext), 1)
    for b in range(nblk):
        count = jnp.zeros((1, ext), F32)
        for n in range(NB):
            first = (adj_ref[b, n] - g * nblk + R_BLK) * QB
            count += jnp.where((col >= first) & (col < first + QB), 1.0, 0.0)
        rows = jnp.broadcast_to(count, (QB, ext))
        cnt_s[b * QB : (b + 1) * QB] = rows
        cnt_s[points + b * QB : points + (b + 1) * QB] = rows

    w_copy.wait()
    tile = 512

    @pl.loop(0, width // tile)
    def _(t):
        own = nrm[:, RIM : RIM + points].reshape(members * points, width)
        c = pl.multiple_of(t * tile, tile)
        q_s[:, :, pl.ds(c, tile)] = mm(own, w_ref[:, pl.ds(c, tile)]).astype(BF16).reshape(
            members, points, tile
        )

    @pl.loop(0, 2 * width // tile)
    def _(t):
        own = nrm[:, RIM : RIM + points].reshape(members * points, width)
        c = pl.multiple_of(t * tile, tile)
        wt = w_ref[:, pl.ds(pl.multiple_of(c + width, tile), tile)]
        kv[:, RIM : RIM + points, pl.ds(c, tile)] = mm(own, wt).astype(BF16).reshape(
            members, points, tile
        )

    head_a = lax.broadcasted_iota(jnp.int32, (points, LANES), 1) < LANES // 2

    def stacked(v):
        zero = jnp.zeros_like(v)
        return jnp.concatenate([jnp.where(head_a, v, zero), jnp.where(head_a, zero, v)], axis=0)

    def merged(v):
        return jnp.where(head_a, v[:points], v[points:])

    group = 2

    def cols(c):
        c = pl.multiple_of(c * LANES, LANES)
        return pl.ds(c, LANES), pl.ds(pl.multiple_of(c + width, LANES), LANES)

    sends = []
    for m in range(members):
        pl.when(g > 0)(ups[m].wait_recv)
        pl.when(g < n_grid - 1)(downs[m].wait_recv)

        @pl.loop(0, 2 * width // tile)
        def _(t):
            c = pl.multiple_of(t * tile, tile)
            wt = w_ref[:, pl.ds(pl.multiple_of(c + width, tile), tile)]
            rim = jnp.concatenate([nrm[m, :RIM], nrm[m, RIM + points :]], axis=0)
            res = mm(rim, wt).astype(BF16)
            kv[m, :RIM, pl.ds(c, tile)] = res[:RIM]
            kv[m, RIM + points :, pl.ds(c, tile)] = res[RIM:]

        @pl.loop(0, pairs // group)
        def _(it):
            cnt = cnt_s[...]
            at = [cols(it * group + i) for i in range(group)]
            ss = [mm_nt(stacked(q_s[m, :, ck]), kv[m, :, ck]) for ck, _ in at]
            ss = [jnp.where(cnt > 0.0, s * scale, NEG) for s in ss]
            ex = [jnp.exp(s - jnp.max(s, axis=-1, keepdims=True)) * cnt for s in ss]
            aa = [x * (1.0 / jnp.sum(x, axis=-1, keepdims=True)) for x in ex]
            res = [merged(mm(a.astype(BF16), kv[m, :, cv])) for a, (_, cv) in zip(aa, at)]
            for i in range(group):
                ac_s[m * pairs + it * group + i] = aa[i]
                state[m, :, at[i][0]] = res[i]

        st = x_ref[m].astype(F32) + state[m]
        state[m] = st
        h = (st * rms_scale(st)).astype(BF16)
        hid[m * points : (m + 1) * points] = h
        fc[e, m] = mm_nt(h, rt[...])
        for k in range(1, n_ens):
            i = m * n_ens + k
            cp = ens_copy(fc.at[e, m], fc.at[e, m], fc_send.at[i], fc_recv.at[i], (e + k) % n_ens)
            cp.start()
            sends.append(cp)

    @pl.loop(0, members * pairs)
    def _(it):
        ac_t[it] = ac_s[it].astype(BF16).T

    for m in range(members):
        nrm_t[m] = nrm[m].T
    hid_t[...] = hid[...].T

    for cp in sends:
        cp.wait()

    lane = lax.broadcasted_iota(jnp.int32, (1, LANES), 1)
    valid = lane < channels
    total = jnp.zeros((1, LANES), F32)
    g16 = []
    for m in range(members):
        parts = []
        for j in range(patches):
            rows = slice(j * SCORED_ENTRIES, (j + 1) * SCORED_ENTRIES)
            rnd = (lane + g * patches + j) % rounds
            partner = jnp.zeros((1, LANES), jnp.int32)
            for r in range(rounds):
                partner = jnp.where(rnd == r, comp_ref[r, e * members + m], partner)
            f = fc[e, m, rows]
            pf = jnp.zeros_like(f)
            for n in range(n_ens * members):
                pf = jnp.where(partner == n, fc[n // members, n % members, rows], pf)
            wgt = wgts[rows]
            err = f - tgt[rows]
            dif = f - pf
            dt = jnp.sqrt(jnp.sum(wgt * err * err, axis=0, keepdims=True) + EPSILON)
            dp = jnp.sqrt(jnp.sum(wgt * dif * dif, axis=0, keepdims=True) + EPSILON)
            total += jnp.where(valid, dt - 0.5 * dp, 0.0)
            parts.append((wgt * err / dt - wgt * dif / dp).astype(BF16))
        g16.append(jnp.concatenate(parts, axis=0) if patches > 1 else parts[0])
    g_all = jnp.concatenate(g16, axis=0)

    tq[e] = jnp.broadcast_to(jnp.sum(total, axis=-1, keepdims=True), (8, LANES))
    tqs = []
    for k in range(1, n_ens):
        cp = ens_copy(tq.at[e], tq.at[e], tq_send.at[k], tq_recv.at[k], (e + k) % n_ens)
        cp.start()
        tqs.append(cp)

    for m in range(members):
        gh = mm(g16[m], rt[...])
        st = state[m]
        inv = rms_scale(st)
        y = st * inv
        gs = inv * (gh - y * jnp.mean(gh * y, axis=-1, keepdims=True))
        out_ref[m] = gs
        go[m] = gs.astype(BF16)

    for m in range(members):
        @pl.loop(0, pairs // group)
        def _(it):
            at = [cols(it * group + i) for i in range(group)]
            res = [mm(ac_t[m * pairs + it * group + i], stacked(go[m, :, at[i][0]])).astype(BF16)
                   for i in range(group)]
            for i in range(group):
                gkv[m, :, at[i][1]] = res[i]

    per_ens = width // n_ens

    def folded(v, count):
        v = v.reshape(n_grid, rows_pp, count)
        if fold > 1:
            step = count // fold
            v = jnp.concatenate([v[:, :, i * step : (i + 1) * step] for i in range(fold)], axis=1)
        return v.astype(BF16)

    @pl.loop(0, n_ens)
    def _(qd):
        d = pl.ds(pl.multiple_of(qd * per_ens, per_ens), per_ens)
        acc = mm(nrm_t[0, d], gkv[0, :, width:])
        for m in range(1, members):
            acc += mm(nrm_t[m, d], gkv[m, :, width:])
        vp[qd, :, :, :wide] = folded(acc, width)
        dec = mm(hid_t[d], g_all)
        if fold > 1:
            dec = jnp.concatenate(
                [dec, jnp.zeros((per_ens, LANES * (fold - 1)), F32)], axis=1
            )
        vp[qd, :, :, wide:] = folded(dec, LANES * fold)

    cores = []
    for k in range(n_far):
        f = (far + 1 + k) % n_far
        cp = ens_copy(vp.at[2 * f + 1 - core], rc0.at[f], core_send.at[k], core_recv.at[k],
                      2 * far + 1 - core)
        cp.start()
        cores.append(cp)

    for cp in tqs:
        cp.wait()
    tg[g] = functools.reduce(lambda a, b: a + b, [tq[i] for i in range(n_ens)])
    tgs = []
    for k in range(1, n_grid):
        cp = grid_copy(tg.at[g], tg.at[g], tg_send.at[k], tg_recv.at[k], (g + k) % n_grid)
        cp.start()
        tgs.append(cp)

    def back(m, start, stop):
        @pl.loop(start, stop)
        def _(it):
            at = [cols(it * group + i) for i in range(group)]
            aa = [ac_s[m * pairs + it * group + i] for i in range(group)]
            da = [mm_nt(stacked(go[m, :, ck]), kv[m, :, cv]) for ck, cv in at]
            ds = [a * (d - jnp.sum(a * d, axis=-1, keepdims=True)) * scale for a, d in zip(aa, da)]
            ds = [d.astype(BF16) for d in ds]
            dq = [merged(mm(d, kv[m, :, ck])).astype(BF16) for d, (ck, _) in zip(ds, at)]
            dk = [mm_tn(d, stacked(q_s[m, :, ck])).astype(BF16) for d, (ck, _) in zip(ds, at)]
            for i in range(group):
                gq[m, :, at[i][0]] = dq[i]
                gkv[m, :, at[i][0]] = dk[i]

    dt_tile = 256

    to_prev, to_next = [], []

    def rim_back(m):
        @pl.loop(0, width // dt_tile)
        def _(t):
            d = pl.ds(pl.multiple_of(t * dt_tile, dt_tile), dt_tile)
            rim = jnp.concatenate([gkv[m, :RIM], gkv[m, RIM + points :]], axis=0)
            res = mm_nt(rim, w_ref[d, width:]).astype(BF16)
            gnr[m, :, :, d] = res.reshape(2, RIM, dt_tile)

        prev = grid_copy(gnr.at[m, 0], gnx.at[m, 0], back_send.at[m], back_recv.at[m],
                         (g + n_grid - 1) % n_grid)
        nxt = grid_copy(gnr.at[m, 1], gnx.at[m, 1], back_send.at[members + m],
                        back_recv.at[members + m], (g + 1) % n_grid)
        pl.when(g > 0)(prev.start)
        pl.when(g < n_grid - 1)(nxt.start)
        to_prev.append(prev)
        to_next.append(nxt)

    xs = []

    def far_stage():
        for k in range(n_far - 1):
            cores[k].wait()
            f = (far + 1 + k) % n_far
            for c in range(pieces):
                sl = pl.ds(c * per_piece, per_piece)
                s1[k, sl] = (vp[2 * f + core, sl].astype(F32) + rc0[f, sl].astype(F32)).astype(BF16)
                cp = ens_copy(s1.at[k, sl], rc1.at[k, sl], x_send.at[k * pieces + c],
                              x_recv.at[k * pieces + c], 2 * f + core)
                cp.start()
                xs.append(cp)
        cores[n_far - 1].wait()

    gcs = [
        grid_copy(s2.at[(g + k) % n_grid], r2.at[k], g_send.at[k], g_recv.at[k], (g + k) % n_grid)
        for k in range(1, n_grid)
    ]

    def grid_stage(c):
        lo = c * per_piece
        sl = pl.ds(lo, per_piece)
        part = vp[2 * far + core, sl].astype(F32) + rc0[far, sl].astype(F32)
        for k in range(n_far - 1):
            xs[k * pieces + c].wait()
            part += rc1[k, sl].astype(F32)
        s2[sl] = part.astype(BF16)
        for k in range(1, n_grid):
            to = (g + k) % n_grid
            pl.when((to >= lo) & (to < lo + per_piece))(gcs[k - 1].start)

    steps = pairs // group
    for m in range(members):
        if m == 0:
            back(m, 0, 1)
            far_stage()
            back(m, 1, steps)
        elif m == 1:
            grid_stage(0)
            back(m, 0, steps // 2)
            for c in range(1, pieces):
                grid_stage(c)
            back(m, steps // 2, steps)
        else:
            back(m, 0, steps)
        rim_back(m)
    if members == 1:
        for c in range(pieces):
            grid_stage(c)

    @pl.loop(0, width // dt_tile)
    def _(t):
        d = pl.ds(pl.multiple_of(t * dt_tile, dt_tile), dt_tile)
        res = mm_nt(gq[...].reshape(members * points, width), w_ref[d, :width])
        res += mm_nt(gkv[:, RIM : RIM + points].reshape(members * points, 2 * width),
                     w_ref[d, width:])
        state[:, :, d] = res.reshape(members, points, dt_tile)

    for cp in tgs:
        cp.wait()
    whole = functools.reduce(lambda a, b: a + b, [tg[i] for i in range(n_grid)])
    count = n_ens * members * channels * patches * n_grid
    tot_ref[...] = whole * (1.0 / count)

    for m in range(members):
        @pl.when(g < n_grid - 1)
        def _():
            to_prev[m].wait_recv()
            state[m, points - RIM :] += gnx[m, 0].astype(F32)

        @pl.when(g > 0)
        def _():
            to_next[m].wait_recv()
            state[m, :RIM] += gnx[m, 1].astype(F32)

        lat = x_ref[m].astype(F32)
        inv = rms_scale(lat)
        y = lat * inv
        gn = state[m]
        out_ref[m] += inv * (gn - y * jnp.mean(gn * y, axis=-1, keepdims=True))

    for cp in gcs:
        cp.wait()
    acc = s2[g].astype(F32)
    for k in range(1, n_grid):
        acc += r2[k].astype(F32)
    for i in range(fold):
        for c in range(wide // LANES):
            gv_ref[:, i * (wide // LANES) + c] = acc[
                i * rows_pp : (i + 1) * rows_pp, c * LANES : (c + 1) * LANES
            ]
    gd_ref[...] = acc[:rows_pp, wide:]

    for m in range(members):
        @pl.when(g < n_grid - 1)
        def _():
            ups[m].wait_send()
            to_next[m].wait_send()

        @pl.when(g > 0)
        def _():
            downs[m].wait_send()
            to_prev[m].wait_send()


def per_device(
    embeddings,
    reference_analysis,
    attention_matrix,
    readout_matrix,
    adjacent_blocks,
    companion_matrix,
    continent_indicator,
    zonal_strip,
):
    members, points, width = embeddings.shape
    channels = reference_analysis.shape[0]
    n_ens, n_grid = lax.axis_size("ens"), lax.axis_size("grid")
    ext = points + 2 * RIM
    pairs = width // LANES
    rows_pp = width // (n_ens * n_grid)
    fold = max(1, 16 // rows_pp)
    chunk = (rows_pp * fold, width // fold + LANES)
    n_far = n_ens // 2
    patches = points // SCORED_ENTRIES
    pieces = 2 if n_grid % 2 == 0 else 1
    vmem = pl.BlockSpec(memory_space=pltpu.VMEM)
    smem = pl.BlockSpec(memory_space=pltpu.SMEM)
    dma = pltpu.SemaphoreType.DMA
    V = pltpu.VMEM
    scratch = [
        V((width, 3 * width), BF16),
        V((LANES, width), BF16),
        V((points, LANES), F32),
        V((points, LANES), F32),
        V((members, ext, width), BF16),
        V((members, width, ext), BF16),
        V((members, points, width), BF16),
        V((members, ext, 2 * width), BF16),
        V((2 * points, ext), F32),
        V((members * pairs, 2 * points, ext), F32),
        V((members * pairs, ext, 2 * points), BF16),
        V((members, points, width), F32),
        V((members * points, width), BF16),
        V((width, members * points), BF16),
        V((members, points, width), BF16),
        V((members, points, width), BF16),
        V((members, ext, 2 * width), BF16),
        V((n_ens, members, points, LANES), F32),
        V((n_ens, n_grid) + chunk, BF16),
        V((n_far, n_grid) + chunk, BF16),
        V((max(1, n_far - 1), n_grid) + chunk, BF16),
        V((max(1, n_far - 1), n_grid) + chunk, BF16),
        V((n_grid,) + chunk, BF16),
        V((n_grid,) + chunk, BF16),
        V((members, 2, RIM, width), BF16),
        V((members, 2, RIM, width), BF16),
        V((n_ens, 8, LANES), F32),
        V((n_grid, 8, LANES), F32),
        dma(()),
        dma((2 * members,)), dma((2 * members,)),
        dma((members * n_ens,)), dma((members * n_ens,)),
        dma((n_far,)), dma((n_far,)),
        dma((n_far * pieces,)), dma((n_far * pieces,)),
        dma((n_grid,)), dma((n_grid,)),
        dma((2 * members,)), dma((2 * members,)),
        dma((n_ens,)), dma((n_ens,)),
        dma((n_grid,)), dma((n_grid,)),
    ]
    total, sens, grad_value, grad_dec = pl.pallas_call(
        functools.partial(kernel, n_ens, n_grid, channels),
        out_shape=(
            jax.ShapeDtypeStruct((8, LANES), F32),
            jax.ShapeDtypeStruct((members, points, width), F32),
            jax.ShapeDtypeStruct((rows_pp, width // LANES, LANES), F32),
            jax.ShapeDtypeStruct((rows_pp, LANES), F32),
        ),
        in_specs=[smem, smem, vmem, vmem, pl.BlockSpec(memory_space=pl.ANY), vmem, vmem, vmem],
        out_specs=(vmem,) * 4,
        scratch_shapes=scratch,
        compiler_params=pltpu.CompilerParams(
            collective_id=0, has_side_effects=True, vmem_limit_bytes=60 * 1024 * 1024
        ),
    )(
        adjacent_blocks,
        companion_matrix,
        embeddings,
        reference_analysis,
        attention_matrix,
        readout_matrix.T,
        continent_indicator.reshape(patches, SCORED_ENTRIES),
        zonal_strip.reshape(patches, SCORED_ENTRIES),
    )
    return (
        total[0, 0],
        sens,
        grad_value.reshape(-1),
        grad_dec[:, :channels].reshape(-1),
    )


def solution(mesh):
    in_specs = (
        P("ens", "grid", None),
        P(None, "grid"),
        P(),
        P(),
        P("grid", None),
        P(),
        P("grid"),
        P("grid"),
    )
    out_specs = (P(), P("ens", "grid", None), P(("ens", "grid")), P(("ens", "grid")))
    return jax.shard_map(
        per_device, mesh=mesh, in_specs=in_specs, out_specs=out_specs, check_vma=False
    )
```

```python
import functools
import math

import jax
import jax.numpy as jnp
from jax import lax
from jax.experimental import pallas as pl
from jax.experimental.pallas import tpu as pltpu
from jax.sharding import PartitionSpec as P

HEADS = 16
QB = 64
R_BLK = 2
NB = 3
SCORED_ENTRIES = 128
NLAT = 721
EPSILON = 1e-06
RIM = R_BLK * QB
LANES = 128
NEG = -1e30

F32 = jnp.float32
BF16 = jnp.bfloat16
MESH = pl.DeviceIdType.MESH


def mm(a, b):
    return lax.dot_general(a, b, (((1,), (0,)), ((), ())), preferred_element_type=F32)


def mm_nt(a, b):
    return lax.dot_general(a, b, (((1,), (1,)), ((), ())), preferred_element_type=F32)


def mm_tn(a, b):
    return lax.dot_general(a, b, (((0,), (0,)), ((), ())), preferred_element_type=F32)


def rms_scale(values):
    return lax.rsqrt(jnp.mean(values * values, axis=-1, keepdims=True) + EPSILON)


def kernel(
    n_ens, n_grid, channels,
    adj_ref, comp_ref, x_ref, ref_ref, w_hbm, r_ref, land_ref, strip_ref,
    tot_ref, out_ref, gv_ref, gd_ref,
    w_ref, rt, tgt, wgts, nrm, nrm_t, q_s, kv, cnt_s, ac_s, ac_t, state, hid, hid_t, go, gq, gkv, fc,
    vp, rc0, s1, rc1, s2, r2, gnr, gx, hand, gnx, ds_s, tq, tg,
    w_sem, halo_send, halo_recv, fc_send, fc_recv, core_send, core_recv,
    x_send, x_recv, g_send, g_recv, back_send, back_recv,
    tq_send, tq_recv, tg_send, tg_recv,
):
    members, points, width = x_ref.shape
    ext = points + 2 * RIM
    nblk = points // QB
    pairs = width // LANES
    rounds = comp_ref.shape[0]
    patches = points // SCORED_ENTRIES
    rows_pp = width // (n_ens * n_grid)
    fold = max(1, 16 // rows_pp)
    wide = width // fold
    n_far = n_ens // 2
    pieces = 2 if n_grid % 2 == 0 else 1
    per_piece = n_grid // pieces
    e = lax.axis_index("ens")
    g = lax.axis_index("grid")
    core = e % 2
    far = e // 2
    scale = 1.0 / math.sqrt(width // HEADS)

    def ens_copy(src, dst, ss, rs, to):
        return pltpu.make_async_remote_copy(
            src_ref=src, dst_ref=dst, send_sem=ss, recv_sem=rs,
            device_id={"ens": to}, device_id_type=MESH,
        )

    def grid_copy(src, dst, ss, rs, to):
        return pltpu.make_async_remote_copy(
            src_ref=src, dst_ref=dst, send_sem=ss, recv_sem=rs,
            device_id={"grid": to}, device_id_type=MESH,
        )

    w_copy = pltpu.make_async_copy(w_hbm, w_ref, w_sem)
    w_copy.start()
    barrier = pltpu.get_barrier_semaphore()
    for k in range(1, n_ens):
        pl.semaphore_signal(barrier, inc=1, device_id={"ens": (e + k) % n_ens}, device_id_type=MESH)
    for k in range(1, n_grid):
        pl.semaphore_signal(barrier, inc=1, device_id={"grid": (g + k) % n_grid}, device_id_type=MESH)

    @pl.when(g == 0)
    def _():
        nrm[:, :RIM] = jnp.zeros((members, RIM, width), BF16)

    @pl.when(g == n_grid - 1)
    def _():
        nrm[:, RIM + points :] = jnp.zeros((members, RIM, width), BF16)

    odd = g % 2
    far_row = RIM + points
    near_src = pl.ds(pl.multiple_of((1 - odd) * far_row, RIM), RIM)
    away = pl.ds(pl.multiple_of(odd * far_row, RIM), RIM)
    mate = g + 1 - 2 * odd
    onward = g + 2 - 4 * odd
    back_to = g - 2 + 4 * odd
    has_onward = (onward >= 0) & (onward < n_grid)
    has_back = (back_to >= 0) & (back_to < n_grid)
    onward_id = (onward + n_grid) % n_grid
    back_id = (back_to + n_grid) % n_grid
    swaps, passes = [], []
    for m in range(members):
        lat = x_ref[m].astype(F32)
        nrm[m, RIM : RIM + points] = (lat * rms_scale(lat)).astype(BF16)
        if m == 0:
            pl.semaphore_wait(barrier, n_ens + n_grid - 2)
        cp = grid_copy(nrm.at[m, pl.ds(RIM, RIM)], nrm.at[m, away],
                       halo_send.at[m], halo_recv.at[m], mate)
        cp.start()
        swaps.append(cp)
        passes.append(grid_copy(nrm.at[m, near_src], nrm.at[m, away],
                                halo_send.at[members + m], halo_recv.at[members + m], onward_id))

    def pass_on(m):
        swaps[m].wait_recv()
        pl.when(has_onward)(passes[m].start)

    out_ref[...] = jnp.zeros(out_ref.shape, F32)
    out_ref[0, :channels] = r_ref[...].astype(F32)
    out_ref[1, :channels, :points] = ref_ref[...]
    rt[...] = out_ref[0, :LANES].astype(BF16)
    for j in range(patches):
        rows = slice(j * SCORED_ENTRIES, (j + 1) * SCORED_ENTRIES)
        tgt[rows] = out_ref[1, :LANES, rows].T
        phase = (strip_ref[j : j + 1].astype(F32) + 0.5) * (math.pi / NLAT) - 0.5 * math.pi
        wrow = jnp.cos(phase) * (1.0 + land_ref[j : j + 1].astype(F32))
        wgts[rows] = jnp.broadcast_to(wrow, (LANES, SCORED_ENTRIES)).T

    col = lax.broadcasted_iota(jnp.int32, (1, ext), 1)
    for b in range(nblk):
        count = jnp.zeros((1, ext), F32)
        for n in range(NB):
            first = (adj_ref[b, n] - g * nblk + R_BLK) * QB
            count += jnp.where((col >= first) & (col < first + QB), 1.0, 0.0)
        rows = jnp.broadcast_to(count, (QB, ext))
        cnt_s[b * QB : (b + 1) * QB] = rows
        cnt_s[points + b * QB : points + (b + 1) * QB] = rows

    w_copy.wait()
    tile = 512

    @pl.loop(0, width // tile)
    def _(t):
        own = nrm[:, RIM : RIM + points].reshape(members * points, width)
        c = pl.multiple_of(t * tile, tile)
        q_s[:, :, pl.ds(c, tile)] = mm(own, w_ref[:, pl.ds(c, tile)]).astype(BF16).reshape(
            members, points, tile
        )

    pass_on(0)

    @pl.loop(0, 2 * width // tile)
    def _(t):
        own = nrm[:, RIM : RIM + points].reshape(members * points, width)
        c = pl.multiple_of(t * tile, tile)
        wt = w_ref[:, pl.ds(pl.multiple_of(c + width, tile), tile)]
        kv[:, RIM : RIM + points, pl.ds(c, tile)] = mm(own, wt).astype(BF16).reshape(
            members, points, tile
        )

    for m in range(1, members):
        pass_on(m)

    @pl.loop(0, 2 * width // tile)
    def _(t):
        near = nrm[:, near_src].reshape(members * RIM, width)
        c = pl.multiple_of(t * tile, tile)
        wt = w_ref[:, pl.ds(pl.multiple_of(c + width, tile), tile)]
        kv[:, near_src, pl.ds(c, tile)] = mm(near, wt).astype(BF16).reshape(members, RIM, tile)

    head_a = lax.broadcasted_iota(jnp.int32, (points, LANES), 1) < LANES // 2

    def stacked(v):
        zero = jnp.zeros_like(v)
        return jnp.concatenate([jnp.where(head_a, v, zero), jnp.where(head_a, zero, v)], axis=0)

    def merged(v):
        return jnp.where(head_a, v[:points], v[points:])

    group = 2

    def cols(c):
        c = pl.multiple_of(c * LANES, LANES)
        return pl.ds(c, LANES), pl.ds(pl.multiple_of(c + width, LANES), LANES)

    sends = []
    for m in range(members):
        pl.when(has_back)(passes[m].wait_recv)

        @pl.loop(0, 2 * width // tile)
        def _(t):
            c = pl.multiple_of(t * tile, tile)
            wt = w_ref[:, pl.ds(pl.multiple_of(c + width, tile), tile)]
            kv[m, away, pl.ds(c, tile)] = mm(nrm[m, away], wt).astype(BF16)

        @pl.loop(0, pairs // group)
        def _(it):
            cnt = cnt_s[...]
            at = [cols(it * group + i) for i in range(group)]
            ss = [mm_nt(stacked(q_s[m, :, ck]), kv[m, :, ck]) for ck, _ in at]
            ss = [jnp.where(cnt > 0.0, s * scale, NEG) for s in ss]
            ex = [jnp.exp(s - jnp.max(s, axis=-1, keepdims=True)) * cnt for s in ss]
            aa = [x * (1.0 / jnp.sum(x, axis=-1, keepdims=True)) for x in ex]
            res = [merged(mm(a.astype(BF16), kv[m, :, cv])) for a, (_, cv) in zip(aa, at)]
            for i in range(group):
                ac_s[m * pairs + it * group + i] = aa[i]
                state[m, :, at[i][0]] = res[i]

        st = x_ref[m].astype(F32) + state[m]
        state[m] = st
        h = (st * rms_scale(st)).astype(BF16)
        hid[m * points : (m + 1) * points] = h
        fc[e, m] = mm_nt(h, rt[...])
        for k in range(1, n_ens):
            i = m * n_ens + k
            cp = ens_copy(fc.at[e, m], fc.at[e, m], fc_send.at[i], fc_recv.at[i], (e + k) % n_ens)
            cp.start()
            sends.append(cp)

    @pl.loop(0, members * pairs)
    def _(it):
        ac_t[it] = ac_s[it].astype(BF16).T

    for m in range(members):
        nrm_t[m] = nrm[m].T
    hid_t[...] = hid[...].T

    for cp in sends:
        cp.wait()

    lane = lax.broadcasted_iota(jnp.int32, (1, LANES), 1)
    valid = lane < channels
    total = jnp.zeros((1, LANES), F32)
    g16 = []
    for m in range(members):
        parts = []
        for j in range(patches):
            rows = slice(j * SCORED_ENTRIES, (j + 1) * SCORED_ENTRIES)
            rnd = (lane + g * patches + j) % rounds
            partner = jnp.zeros((1, LANES), jnp.int32)
            for r in range(rounds):
                partner = jnp.where(rnd == r, comp_ref[r, e * members + m], partner)
            f = fc[e, m, rows]
            pf = jnp.zeros_like(f)
            for n in range(n_ens * members):
                pf = jnp.where(partner == n, fc[n // members, n % members, rows], pf)
            wgt = wgts[rows]
            err = f - tgt[rows]
            dif = f - pf
            dt = jnp.sqrt(jnp.sum(wgt * err * err, axis=0, keepdims=True) + EPSILON)
            dp = jnp.sqrt(jnp.sum(wgt * dif * dif, axis=0, keepdims=True) + EPSILON)
            total += jnp.where(valid, dt - 0.5 * dp, 0.0)
            parts.append((wgt * err / dt - wgt * dif / dp).astype(BF16))
        g16.append(jnp.concatenate(parts, axis=0) if patches > 1 else parts[0])
    g_all = jnp.concatenate(g16, axis=0)

    tq[e] = jnp.broadcast_to(jnp.sum(total, axis=-1, keepdims=True), (8, LANES))
    tqs = []
    for k in range(1, n_ens):
        cp = ens_copy(tq.at[e], tq.at[e], tq_send.at[k], tq_recv.at[k], (e + k) % n_ens)
        cp.start()
        tqs.append(cp)

    for m in range(members):
        gh = mm(g16[m], rt[...])
        st = state[m]
        inv = rms_scale(st)
        y = st * inv
        gs = inv * (gh - y * jnp.mean(gh * y, axis=-1, keepdims=True))
        out_ref[m] = gs
        go[m] = gs.astype(BF16)

    for m in range(members):
        @pl.loop(0, pairs // group)
        def _(it):
            at = [cols(it * group + i) for i in range(group)]
            res = [mm(ac_t[m * pairs + it * group + i], stacked(go[m, :, at[i][0]])).astype(BF16)
                   for i in range(group)]
            for i in range(group):
                gkv[m, :, at[i][1]] = res[i]

    per_ens = width // n_ens

    def folded(v, count):
        v = v.reshape(n_grid, rows_pp, count)
        if fold > 1:
            step = count // fold
            v = jnp.concatenate([v[:, :, i * step : (i + 1) * step] for i in range(fold)], axis=1)
        return v.astype(BF16)

    @pl.loop(0, n_ens)
    def _(qd):
        d = pl.ds(pl.multiple_of(qd * per_ens, per_ens), per_ens)
        acc = mm(nrm_t[0, d], gkv[0, :, width:])
        for m in range(1, members):
            acc += mm(nrm_t[m, d], gkv[m, :, width:])
        vp[qd, :, :, :wide] = folded(acc, width)
        dec = mm(hid_t[d], g_all)
        if fold > 1:
            dec = jnp.concatenate(
                [dec, jnp.zeros((per_ens, LANES * (fold - 1)), F32)], axis=1
            )
        vp[qd, :, :, wide:] = folded(dec, LANES * fold)

    cores = []
    for k in range(n_far):
        f = (far + 1 + k) % n_far
        cp = ens_copy(vp.at[2 * f + 1 - core], rc0.at[f], core_send.at[k], core_recv.at[k],
                      2 * far + 1 - core)
        cp.start()
        cores.append(cp)

    for cp in tqs:
        cp.wait()
    tg[g] = functools.reduce(lambda a, b: a + b, [tq[i] for i in range(n_ens)])
    tgs = []
    for k in range(1, n_grid):
        cp = grid_copy(tg.at[g], tg.at[g], tg_send.at[k], tg_recv.at[k], (g + k) % n_grid)
        cp.start()
        tgs.append(cp)

    def back(m, start, stop):
        @pl.loop(start, stop)
        def _(it):
            at = [cols(it * group + i) for i in range(group)]
            aa = [ac_s[m * pairs + it * group + i] for i in range(group)]
            da = [mm_nt(stacked(go[m, :, ck]), kv[m, :, cv]) for ck, cv in at]
            ds = [a * (d - jnp.sum(a * d, axis=-1, keepdims=True)) * scale for a, d in zip(aa, da)]
            ds = [d.astype(BF16) for d in ds]
            dk = [mm_tn(d, stacked(q_s[m, :, ck])).astype(BF16) for d, (ck, _) in zip(ds, at)]
            for i in range(group):
                ds_s[m * pairs + it * group + i] = ds[i]
                gkv[m, :, at[i][0]] = dk[i]

    def back_query(m):
        @pl.loop(0, pairs // group)
        def _(it):
            at = [cols(it * group + i) for i in range(group)]
            dq = [merged(mm(ds_s[m * pairs + it * group + i], kv[m, :, at[i][0]])).astype(BF16)
                  for i in range(group)]
            for i in range(group):
                gq[m, :, at[i][0]] = dq[i]

    dt_tile = 256

    crosses = [
        grid_copy(gnr.at[m, odd], gx.at[m], back_send.at[m], back_recv.at[m], back_id)
        for m in range(members)
    ]
    hands = [
        grid_copy(hand.at[m], gnx.at[m], back_send.at[members + m], back_recv.at[members + m], mate)
        for m in range(members)
    ]

    def rim_back(m):
        @pl.loop(0, width // dt_tile)
        def _(t):
            d = pl.ds(pl.multiple_of(t * dt_tile, dt_tile), dt_tile)
            rim = jnp.concatenate([gkv[m, :RIM], gkv[m, RIM + points :]], axis=0)
            res = mm_nt(rim, w_ref[d, width:]).astype(BF16)
            gnr[m, :, :, d] = res.reshape(2, RIM, dt_tile)

        pl.when(has_back)(crosses[m].start)

    def hand_over(m):
        hand[m] = gnr[m, 1 - odd]

        @pl.when(has_onward)
        def _():
            crosses[m].wait_recv()
            hand[m] = (gnr[m, 1 - odd].astype(F32) + gx[m].astype(F32)).astype(BF16)

        hands[m].start()

    xs = []

    def far_stage():
        for k in range(n_far - 1):
            cores[k].wait()
            f = (far + 1 + k) % n_far
            for c in range(pieces):
                sl = pl.ds(c * per_piece, per_piece)
                s1[k, sl] = (vp[2 * f + core, sl].astype(F32) + rc0[f, sl].astype(F32)).astype(BF16)
                cp = ens_copy(s1.at[k, sl], rc1.at[k, sl], x_send.at[k * pieces + c],
                              x_recv.at[k * pieces + c], 2 * f + core)
                cp.start()
                xs.append(cp)
        cores[n_far - 1].wait()

    gcs = [
        grid_copy(s2.at[(g + k) % n_grid], r2.at[k], g_send.at[k], g_recv.at[k], (g + k) % n_grid)
        for k in range(1, n_grid)
    ]

    def grid_stage(c):
        lo = c * per_piece
        sl = pl.ds(lo, per_piece)
        part = vp[2 * far + core, sl].astype(F32) + rc0[far, sl].astype(F32)
        for k in range(n_far - 1):
            xs[k * pieces + c].wait()
            part += rc1[k, sl].astype(F32)
        s2[sl] = part.astype(BF16)
        for k in range(1, n_grid):
            to = (g + k) % n_grid
            pl.when((to >= lo) & (to < lo + per_piece))(gcs[k - 1].start)

    steps = pairs // group
    for m in range(members):
        if m == 0:
            back(m, 0, 1)
            far_stage()
            back(m, 1, steps)
        elif m == 1:
            grid_stage(0)
            back(m, 0, steps // 2)
            hand_over(0)
            for c in range(1, pieces):
                grid_stage(c)
            back(m, steps // 2, steps)
        else:
            back(m, 0, steps)
        rim_back(m)
    if members == 1:
        for c in range(pieces):
            grid_stage(c)

    for m in range(members):
        back_query(m)
    for m in range(0 if members == 1 else 1, members):
        hand_over(m)

    @pl.loop(0, width // dt_tile)
    def _(t):
        d = pl.ds(pl.multiple_of(t * dt_tile, dt_tile), dt_tile)
        res = mm_nt(gq[...].reshape(members * points, width), w_ref[d, :width])
        res += mm_nt(gkv[:, RIM : RIM + points].reshape(members * points, 2 * width),
                     w_ref[d, width:])
        state[:, :, d] = res.reshape(members, points, dt_tile)

    for cp in tgs:
        cp.wait()
    whole = functools.reduce(lambda a, b: a + b, [tg[i] for i in range(n_grid)])
    count = n_ens * members * channels * patches * n_grid
    tot_ref[...] = whole * (1.0 / count)

    for m in range(members):
        hands[m].wait_recv()
        lat = x_ref[m].astype(F32)
        inv = rms_scale(lat)
        y = lat * inv
        gn = state[m] + gnx[m].astype(F32)
        out_ref[m] += inv * (gn - y * jnp.mean(gn * y, axis=-1, keepdims=True))

    for cp in gcs:
        cp.wait()
    acc = s2[g].astype(F32)
    for k in range(1, n_grid):
        acc += r2[k].astype(F32)
    for i in range(fold):
        for c in range(wide // LANES):
            gv_ref[:, i * (wide // LANES) + c] = acc[
                i * rows_pp : (i + 1) * rows_pp, c * LANES : (c + 1) * LANES
            ]
    gd_ref[...] = acc[:rows_pp, wide:]

    for m in range(members):
        swaps[m].wait_send()
        hands[m].wait_send()
        pl.when(has_onward)(passes[m].wait_send)
        pl.when(has_back)(crosses[m].wait_send)


def finish(channels, tot_in, sens_in, gv_in, gd_in, tot_ref, sens_ref, gv_ref, gd_ref):
    tot_ref[...] = tot_in[:1, :1]
    sens_ref[...] = sens_in[...]
    gv_ref[...] = gv_in[...]
    if gd_ref.shape[-1] != LANES:
        gd_ref[...] = gd_in[:, :channels]
        return
    for i in range(gd_ref.shape[0]):
        at, parts = i * LANES, []
        while at < (i + 1) * LANES:
            row, c = divmod(at, channels)
            n = min(channels - c, (i + 1) * LANES - at)
            parts.append(gd_in[row : row + 1, c : c + n])
            at += n
        gd_ref[i : i + 1] = jnp.concatenate(parts, axis=1)


def per_device(
    embeddings,
    reference_analysis,
    attention_matrix,
    readout_matrix,
    adjacent_blocks,
    companion_matrix,
    continent_indicator,
    zonal_strip,
):
    members, points, width = embeddings.shape
    channels = reference_analysis.shape[0]
    n_ens, n_grid = lax.axis_size("ens"), lax.axis_size("grid")
    ext = points + 2 * RIM
    pairs = width // LANES
    rows_pp = width // (n_ens * n_grid)
    fold = max(1, 16 // rows_pp)
    chunk = (rows_pp * fold, width // fold + LANES)
    n_far = n_ens // 2
    patches = points // SCORED_ENTRIES
    pieces = 2 if n_grid % 2 == 0 else 1
    assert points == RIM and n_grid % 2 == 0
    vmem = pl.BlockSpec(memory_space=pltpu.VMEM)
    smem = pl.BlockSpec(memory_space=pltpu.SMEM)
    dma = pltpu.SemaphoreType.DMA
    V = pltpu.VMEM
    scratch = [
        V((width, 3 * width), BF16),
        V((LANES, width), BF16),
        V((points, LANES), F32),
        V((points, LANES), F32),
        V((members, ext, width), BF16),
        V((members, width, ext), BF16),
        V((members, points, width), BF16),
        V((members, ext, 2 * width), BF16),
        V((2 * points, ext), F32),
        V((members * pairs, 2 * points, ext), F32),
        V((members * pairs, ext, 2 * points), BF16),
        V((members, points, width), F32),
        V((members * points, width), BF16),
        V((width, members * points), BF16),
        V((members, points, width), BF16),
        V((members, points, width), BF16),
        V((members, ext, 2 * width), BF16),
        V((n_ens, members, points, LANES), F32),
        V((n_ens, n_grid) + chunk, BF16),
        V((n_far, n_grid) + chunk, BF16),
        V((max(1, n_far - 1), n_grid) + chunk, BF16),
        V((max(1, n_far - 1), n_grid) + chunk, BF16),
        V((n_grid,) + chunk, BF16),
        V((n_grid,) + chunk, BF16),
        V((members, 2, RIM, width), BF16),
        V((members, RIM, width), BF16),
        V((members, RIM, width), BF16),
        V((members, RIM, width), BF16),
        V((members * pairs, 2 * points, ext), BF16),
        V((n_ens, 8, LANES), F32),
        V((n_grid, 8, LANES), F32),
        dma(()),
        dma((2 * members,)), dma((2 * members,)),
        dma((members * n_ens,)), dma((members * n_ens,)),
        dma((n_far,)), dma((n_far,)),
        dma((n_far * pieces,)), dma((n_far * pieces,)),
        dma((n_grid,)), dma((n_grid,)),
        dma((2 * members,)), dma((2 * members,)),
        dma((n_ens,)), dma((n_ens,)),
        dma((n_grid,)), dma((n_grid,)),
    ]
    total, sens, grad_value, grad_dec = pl.pallas_call(
        functools.partial(kernel, n_ens, n_grid, channels),
        out_shape=(
            jax.ShapeDtypeStruct((8, LANES), F32),
            jax.ShapeDtypeStruct((members, points, width), F32),
            jax.ShapeDtypeStruct((rows_pp, width // LANES, LANES), F32),
            jax.ShapeDtypeStruct((rows_pp, LANES), F32),
        ),
        in_specs=[smem, smem, vmem, vmem, pl.BlockSpec(memory_space=pl.ANY), vmem, vmem, vmem],
        out_specs=(vmem,) * 4,
        scratch_shapes=scratch,
        compiler_params=pltpu.CompilerParams(
            collective_id=0, has_side_effects=True, vmem_limit_bytes=60 * 1024 * 1024
        ),
    )(
        adjacent_blocks,
        companion_matrix,
        embeddings,
        reference_analysis,
        attention_matrix,
        readout_matrix.T,
        continent_indicator.reshape(patches, SCORED_ENTRIES),
        zonal_strip.reshape(patches, SCORED_ENTRIES),
    )
    flat = rows_pp * channels
    dec_shape = (flat // LANES, LANES) if flat % LANES == 0 else (rows_pp, channels)
    total, sens, grad_value, grad_dec = pl.pallas_call(
        functools.partial(finish, channels),
        out_shape=(
            jax.ShapeDtypeStruct((1, 1), F32),
            jax.ShapeDtypeStruct(sens.shape, F32),
            jax.ShapeDtypeStruct(grad_value.shape, F32),
            jax.ShapeDtypeStruct(dec_shape, F32),
        ),
        in_specs=[vmem] * 4,
        out_specs=(vmem,) * 4,
        compiler_params=pltpu.CompilerParams(vmem_limit_bytes=60 * 1024 * 1024),
    )(total, sens, grad_value, grad_dec)
    return (
        total.reshape(()),
        sens,
        grad_value.reshape(-1),
        grad_dec.reshape(-1),
    )


def solution(mesh):
    in_specs = (
        P("ens", "grid", None),
        P(None, "grid"),
        P(),
        P(),
        P("grid", None),
        P(),
        P("grid"),
        P("grid"),
    )
    out_specs = (P(), P("ens", "grid", None), P(("ens", "grid")), P(("ens", "grid")))
    return jax.shard_map(
        per_device, mesh=mesh, in_specs=in_specs, out_specs=out_specs, check_vma=False
    )
```

```python
import functools
import math

import jax
import jax.numpy as jnp
from jax import lax
from jax.experimental import pallas as pl
from jax.experimental.pallas import tpu as pltpu
from jax.sharding import PartitionSpec as P

HEADS = 16
QB = 64
R_BLK = 2
NB = 3
SCORED_ENTRIES = 128
NLAT = 721
EPSILON = 1e-06
RIM = R_BLK * QB
LANES = 128
NEG = -1e30

F32 = jnp.float32
BF16 = jnp.bfloat16
MESH = pl.DeviceIdType.MESH


def mm(a, b):
    return lax.dot_general(a, b, (((1,), (0,)), ((), ())), preferred_element_type=F32)


def mm_nt(a, b):
    return lax.dot_general(a, b, (((1,), (1,)), ((), ())), preferred_element_type=F32)


def mm_tn(a, b):
    return lax.dot_general(a, b, (((0,), (0,)), ((), ())), preferred_element_type=F32)


def rms_scale(values):
    return lax.rsqrt(jnp.mean(values * values, axis=-1, keepdims=True) + EPSILON)


def kernel(
    n_ens, n_grid, channels,
    adj_ref, comp_ref, x_ref, ref_ref, w_hbm, r_ref, land_ref, strip_ref,
    tot_ref, out_ref, gv_ref, gd_ref,
    w_ref, rt, tgt, wgts, nrm, nrm_t, q_s, kv, lc_s, ac_s, ac_t, state, hid, hid_t, go, gq, gkv, fc,
    vp, rc0, s1, rc1, s2, r2, gnr, gx, hand, gnx, ds_s, tq, tg,
    w_sem, halo_send, halo_recv, fc_send, fc_recv, core_send, core_recv,
    x_send, x_recv, g_send, g_recv, back_send, back_recv,
    tq_send, tq_recv, tg_send, tg_recv,
):
    members, points, width = x_ref.shape
    ext = points + 2 * RIM
    nblk = points // QB
    pairs = width // LANES
    rounds = comp_ref.shape[0]
    patches = points // SCORED_ENTRIES
    rows_pp = width // (n_ens * n_grid)
    fold = max(1, 16 // rows_pp)
    wide = width // fold
    n_far = n_ens // 2
    half = n_grid // 2
    e = lax.axis_index("ens")
    g = lax.axis_index("grid")
    core = e % 2
    far = e // 2
    scale = 1.0 / math.sqrt(width // HEADS)

    def ens_copy(src, dst, ss, rs, to):
        return pltpu.make_async_remote_copy(
            src_ref=src, dst_ref=dst, send_sem=ss, recv_sem=rs,
            device_id={"ens": to}, device_id_type=MESH,
        )

    def grid_copy(src, dst, ss, rs, to):
        return pltpu.make_async_remote_copy(
            src_ref=src, dst_ref=dst, send_sem=ss, recv_sem=rs,
            device_id={"grid": to}, device_id_type=MESH,
        )

    w_copy = pltpu.make_async_copy(w_hbm, w_ref, w_sem)
    w_copy.start()
    barrier = pltpu.get_barrier_semaphore()
    for k in range(1, n_ens):
        pl.semaphore_signal(barrier, inc=1, device_id={"ens": (e + k) % n_ens}, device_id_type=MESH)
    for k in range(1, n_grid):
        pl.semaphore_signal(barrier, inc=1, device_id={"grid": (g + k) % n_grid}, device_id_type=MESH)

    @pl.when(g == 0)
    def _():
        nrm[:, :RIM] = jnp.zeros((members, RIM, width), BF16)

    @pl.when(g == n_grid - 1)
    def _():
        nrm[:, RIM + points :] = jnp.zeros((members, RIM, width), BF16)

    odd = g % 2
    far_row = RIM + points
    near_src = pl.ds(pl.multiple_of((1 - odd) * far_row, RIM), RIM)
    away = pl.ds(pl.multiple_of(odd * far_row, RIM), RIM)
    mate = g + 1 - 2 * odd
    onward = g + 2 - 4 * odd
    back_to = g - 2 + 4 * odd
    has_onward = (onward >= 0) & (onward < n_grid)
    has_back = (back_to >= 0) & (back_to < n_grid)
    onward_id = (onward + n_grid) % n_grid
    back_id = (back_to + n_grid) % n_grid
    swaps, passes = [], []
    for m in range(members):
        lat = x_ref[m].astype(F32)
        nrm[m, RIM : RIM + points] = (lat * rms_scale(lat)).astype(BF16)
        if m == 0:
            pl.semaphore_wait(barrier, n_ens + n_grid - 2)
        cp = grid_copy(nrm.at[m, pl.ds(RIM, RIM)], nrm.at[m, away],
                       halo_send.at[m], halo_recv.at[m], mate)
        cp.start()
        swaps.append(cp)
        passes.append(grid_copy(nrm.at[m, near_src], nrm.at[m, away],
                                halo_send.at[members + m], halo_recv.at[members + m], onward_id))

    def pass_on(m):
        swaps[m].wait_recv()
        pl.when(has_onward)(passes[m].start)

    out_ref[...] = jnp.zeros(out_ref.shape, F32)
    out_ref[0, :channels] = r_ref[...].astype(F32)
    out_ref[1, :channels, :points] = ref_ref[...]
    rt[...] = out_ref[0, :LANES].astype(BF16)
    for j in range(patches):
        rows = slice(j * SCORED_ENTRIES, (j + 1) * SCORED_ENTRIES)
        tgt[rows] = out_ref[1, :LANES, rows].T
        phase = (strip_ref[j : j + 1].astype(F32) + 0.5) * (math.pi / NLAT) - 0.5 * math.pi
        wrow = jnp.cos(phase) * (1.0 + land_ref[j : j + 1].astype(F32))
        wgts[rows] = jnp.broadcast_to(wrow, (LANES, SCORED_ENTRIES)).T

    col = lax.broadcasted_iota(jnp.int32, (1, ext), 1)
    for b in range(nblk):
        count = jnp.zeros((1, ext), F32)
        for n in range(NB):
            first = (adj_ref[b, n] - g * nblk + R_BLK) * QB
            count += jnp.where((col >= first) & (col < first + QB), 1.0, 0.0)
        rows = jnp.where(count > 0.0, jnp.log(jnp.maximum(count, 1.0)), NEG)
        rows = jnp.broadcast_to(rows, (QB, ext))
        lc_s[b * QB : (b + 1) * QB] = rows
        lc_s[points + b * QB : points + (b + 1) * QB] = rows

    w_copy.wait()
    tile = 512

    @pl.loop(0, width // tile)
    def _(t):
        own = nrm[:, RIM : RIM + points].reshape(members * points, width)
        c = pl.multiple_of(t * tile, tile)
        res = mm(own, w_ref[:, pl.ds(c, tile)]).astype(BF16) * scale
        q_s[:, :, pl.ds(c, tile)] = res.astype(BF16).reshape(members, points, tile)

    pass_on(0)

    @pl.loop(0, 2 * width // tile)
    def _(t):
        own = nrm[:, RIM : RIM + points].reshape(members * points, width)
        c = pl.multiple_of(t * tile, tile)
        wt = w_ref[:, pl.ds(pl.multiple_of(c + width, tile), tile)]
        kv[:, RIM : RIM + points, pl.ds(c, tile)] = mm(own, wt).astype(BF16).reshape(
            members, points, tile
        )

    for m in range(1, members):
        pass_on(m)

    @pl.loop(0, 2 * width // tile)
    def _(t):
        near = nrm[:, near_src].reshape(members * RIM, width)
        c = pl.multiple_of(t * tile, tile)
        wt = w_ref[:, pl.ds(pl.multiple_of(c + width, tile), tile)]
        kv[:, near_src, pl.ds(c, tile)] = mm(near, wt).astype(BF16).reshape(members, RIM, tile)

    head_a = lax.broadcasted_iota(jnp.int32, (points, LANES), 1) < LANES // 2

    def stacked(v):
        zero = jnp.zeros_like(v)
        return jnp.concatenate([jnp.where(head_a, v, zero), jnp.where(head_a, zero, v)], axis=0)

    def merged(v):
        return jnp.where(head_a, v[:points], v[points:])

    group = 2

    def cols(c):
        c = pl.multiple_of(c * LANES, LANES)
        return pl.ds(c, LANES), pl.ds(pl.multiple_of(c + width, LANES), LANES)

    sends = []
    for m in range(members):
        pl.when(has_back)(passes[m].wait_recv)

        @pl.loop(0, 2 * width // tile)
        def _(t):
            c = pl.multiple_of(t * tile, tile)
            wt = w_ref[:, pl.ds(pl.multiple_of(c + width, tile), tile)]
            kv[m, away, pl.ds(c, tile)] = mm(nrm[m, away], wt).astype(BF16)

        @pl.loop(0, pairs // group)
        def _(it):
            log_count = lc_s[...]
            at = [cols(it * group + i) for i in range(group)]
            ss = [mm_nt(stacked(q_s[m, :, ck]), kv[m, :, ck]) for ck, _ in at]
            ss = [s + log_count for s in ss]
            ex = [jnp.exp(s - jnp.max(s, axis=-1, keepdims=True)) for s in ss]
            aa = [x * (1.0 / jnp.sum(x, axis=-1, keepdims=True)) for x in ex]
            res = [merged(mm(a.astype(BF16), kv[m, :, cv])) for a, (_, cv) in zip(aa, at)]
            for i in range(group):
                ac_s[m * pairs + it * group + i] = aa[i]
                state[m, :, at[i][0]] = res[i]

        st = x_ref[m].astype(F32) + state[m]
        state[m] = st
        h = (st * rms_scale(st)).astype(BF16)
        hid[m * points : (m + 1) * points] = h
        fc[e, m] = mm_nt(h, rt[...])
        for k in range(1, n_ens):
            i = m * n_ens + k
            cp = ens_copy(fc.at[e, m], fc.at[e, m], fc_send.at[i], fc_recv.at[i], (e + k) % n_ens)
            cp.start()
            sends.append(cp)

    @pl.loop(0, members * pairs)
    def _(it):
        ac_t[it] = ac_s[it].astype(BF16).T

    for m in range(members):
        nrm_t[m] = nrm[m].T
    hid_t[...] = hid[...].T

    for cp in sends:
        cp.wait()

    lane = lax.broadcasted_iota(jnp.int32, (1, LANES), 1)
    valid = lane < channels
    total = jnp.zeros((1, LANES), F32)
    g16 = []
    for m in range(members):
        parts = []
        for j in range(patches):
            rows = slice(j * SCORED_ENTRIES, (j + 1) * SCORED_ENTRIES)
            rnd = (lane + g * patches + j) % rounds
            partner = jnp.zeros((1, LANES), jnp.int32)
            for r in range(rounds):
                partner = jnp.where(rnd == r, comp_ref[r, e * members + m], partner)
            f = fc[e, m, rows]
            pf = jnp.zeros_like(f)
            for n in range(n_ens * members):
                pf = jnp.where(partner == n, fc[n // members, n % members, rows], pf)
            wgt = wgts[rows]
            err = f - tgt[rows]
            dif = f - pf
            dt = jnp.sqrt(jnp.sum(wgt * err * err, axis=0, keepdims=True) + EPSILON)
            dp = jnp.sqrt(jnp.sum(wgt * dif * dif, axis=0, keepdims=True) + EPSILON)
            total += jnp.where(valid, dt - 0.5 * dp, 0.0)
            parts.append((wgt * err / dt - wgt * dif / dp).astype(BF16))
        g16.append(jnp.concatenate(parts, axis=0) if patches > 1 else parts[0])
    g_all = jnp.concatenate(g16, axis=0)

    tq[e] = jnp.broadcast_to(jnp.sum(total, axis=-1, keepdims=True), (8, LANES))
    tqs = []
    for k in range(1, n_ens):
        cp = ens_copy(tq.at[e], tq.at[e], tq_send.at[k], tq_recv.at[k], (e + k) % n_ens)
        cp.start()
        tqs.append(cp)

    for m in range(members):
        gh = mm(g16[m], rt[...])
        st = state[m]
        inv = rms_scale(st)
        y = st * inv
        gs = inv * (gh - y * jnp.mean(gh * y, axis=-1, keepdims=True))
        out_ref[m] = gs
        go[m] = gs.astype(BF16)

    for m in range(members):
        @pl.loop(0, pairs // group)
        def _(it):
            at = [cols(it * group + i) for i in range(group)]
            res = [mm(ac_t[m * pairs + it * group + i], stacked(go[m, :, at[i][0]])).astype(BF16)
                   for i in range(group)]
            for i in range(group):
                gkv[m, :, at[i][1]] = res[i]

    per_ens = width // n_ens

    def folded(v, count):
        v = v.reshape(n_grid, rows_pp, count)
        v = jnp.stack([v[i] for i in list(range(0, n_grid, 2)) + list(range(1, n_grid, 2))])
        if fold > 1:
            step = count // fold
            v = jnp.concatenate([v[:, :, i * step : (i + 1) * step] for i in range(fold)], axis=1)
        return v.astype(BF16)

    @pl.loop(0, n_ens)
    def _(qd):
        d = pl.ds(pl.multiple_of(qd * per_ens, per_ens), per_ens)
        acc = mm(nrm_t[0, d], gkv[0, :, width:])
        for m in range(1, members):
            acc += mm(nrm_t[m, d], gkv[m, :, width:])
        vp[qd, :, :, :wide] = folded(acc, width)
        dec = mm(hid_t[d], g_all)
        if fold > 1:
            dec = jnp.concatenate(
                [dec, jnp.zeros((per_ens, LANES * (fold - 1)), F32)], axis=1
            )
        vp[qd, :, :, wide:] = folded(dec, LANES * fold)

    cores = []
    for k in range(n_far):
        f = (far + 1 + k) % n_far
        cp = ens_copy(vp.at[2 * f + 1 - core], rc0.at[f], core_send.at[k], core_recv.at[k],
                      2 * far + 1 - core)
        cp.start()
        cores.append(cp)

    for cp in tqs:
        cp.wait()
    tg[g] = functools.reduce(lambda a, b: a + b, [tq[i] for i in range(n_ens)])
    tgs = []
    for k in range(1, n_grid):
        cp = grid_copy(tg.at[g], tg.at[g], tg_send.at[k], tg_recv.at[k], (g + k) % n_grid)
        cp.start()
        tgs.append(cp)

    def back(m, start, stop):
        @pl.loop(start, stop)
        def _(it):
            at = [cols(it * group + i) for i in range(group)]
            aa = [ac_s[m * pairs + it * group + i] for i in range(group)]
            da = [mm_nt(stacked(go[m, :, ck]), kv[m, :, cv]) for ck, cv in at]
            ds = [a * (d - jnp.sum(a * d, axis=-1, keepdims=True)) for a, d in zip(aa, da)]
            ds = [d.astype(BF16) for d in ds]
            dk = [mm_tn(d, stacked(q_s[m, :, ck])).astype(BF16) for d, (ck, _) in zip(ds, at)]
            for i in range(group):
                ds_s[m * pairs + it * group + i] = ds[i]
                gkv[m, :, at[i][0]] = dk[i]

    def back_query(m):
        @pl.loop(0, pairs // group)
        def _(it):
            at = [cols(it * group + i) for i in range(group)]
            dq = [merged(mm(ds_s[m * pairs + it * group + i], kv[m, :, at[i][0]])) * scale
                  for i in range(group)]
            for i in range(group):
                gq[m, :, at[i][0]] = dq[i].astype(BF16)

    dt_tile = 256

    crosses = [
        grid_copy(gnr.at[m, odd], gx.at[m], back_send.at[m], back_recv.at[m], back_id)
        for m in range(members)
    ]
    hands = [
        grid_copy(hand.at[m], gnx.at[m], back_send.at[members + m], back_recv.at[members + m], mate)
        for m in range(members)
    ]

    def rim_back(m):
        @pl.loop(0, width // dt_tile)
        def _(t):
            d = pl.ds(pl.multiple_of(t * dt_tile, dt_tile), dt_tile)
            rim = jnp.concatenate([gkv[m, :RIM], gkv[m, RIM + points :]], axis=0)
            res = mm_nt(rim, w_ref[d, width:]).astype(BF16)
            gnr[m, :, :, d] = res.reshape(2, RIM, dt_tile)

        pl.when(has_back)(crosses[m].start)

    def hand_over(m):
        hand[m] = gnr[m, 1 - odd]

        @pl.when(has_onward)
        def _():
            crosses[m].wait_recv()
            hand[m] = (gnr[m, 1 - odd].astype(F32) + gx[m].astype(F32)).astype(BF16)

        hands[m].start()

    xs = []

    def part_of(c):
        return pl.ds(((1 - odd) if c == 0 else odd) * half, half)

    def far_stage():
        for k in range(n_far - 1):
            cores[k].wait()
            f = (far + 1 + k) % n_far
            for c in range(2):
                sl = part_of(c)
                s1[k, sl] = (vp[2 * f + core, sl].astype(F32) + rc0[f, sl].astype(F32)).astype(BF16)
                cp = ens_copy(s1.at[k, sl], rc1.at[k, sl], x_send.at[k * 2 + c],
                              x_recv.at[k * 2 + c], 2 * f + core)
                cp.start()
                xs.append(cp)
        cores[n_far - 1].wait()

    def part_sum(c):
        sl = part_of(c)
        part = vp[2 * far + core, sl].astype(F32) + rc0[far, sl].astype(F32)
        for k in range(n_far - 1):
            xs[k * 2 + c].wait()
            part += rc1[k, sl].astype(F32)
        return part

    mate_copy = grid_copy(s2.at[0], r2.at[0], g_send.at[0], g_recv.at[0], mate)
    place = g // 2
    gcs = [
        grid_copy(s2.at[1, (place + k) % half], r2.at[1, k], g_send.at[k], g_recv.at[k],
                  2 * ((place + k) % half) + odd)
        for k in range(1, half)
    ]

    def mate_stage():
        s2[0] = part_sum(0).astype(BF16)
        mate_copy.start()

    def grid_stage():
        part = part_sum(1)
        mate_copy.wait()
        s2[1] = (part + r2[0].astype(F32)).astype(BF16)
        for cp in gcs:
            cp.start()

    steps = pairs // group
    for m in range(members):
        if m == 0:
            back(m, 0, 1)
            far_stage()
            back(m, 1, steps - 1)
            mate_stage()
            back(m, steps - 1, steps)
        elif m == 1:
            back(m, 0, 1)
            grid_stage()
            back(m, 1, 2)
            hand_over(0)
            back(m, 2, steps)
        else:
            back(m, 0, steps)
        rim_back(m)

    for m in range(members):
        back_query(m)
    for m in range(1, members):
        hand_over(m)

    @pl.loop(0, width // dt_tile)
    def _(t):
        d = pl.ds(pl.multiple_of(t * dt_tile, dt_tile), dt_tile)
        res = mm_nt(gq[...].reshape(members * points, width), w_ref[d, :width])
        res += mm_nt(gkv[:, RIM : RIM + points].reshape(members * points, 2 * width),
                     w_ref[d, width:])
        state[:, :, d] = res.reshape(members, points, dt_tile)

    for cp in tgs:
        cp.wait()
    whole = functools.reduce(lambda a, b: a + b, [tg[i] for i in range(n_grid)])
    count = n_ens * members * channels * patches * n_grid
    tot_ref[...] = whole * (1.0 / count)

    for m in range(members):
        hands[m].wait_recv()
        lat = x_ref[m].astype(F32)
        inv = rms_scale(lat)
        y = lat * inv
        gn = state[m] + gnx[m].astype(F32)
        out_ref[m] += inv * (gn - y * jnp.mean(gn * y, axis=-1, keepdims=True))

    for cp in gcs:
        cp.wait()
    acc = s2[1, place].astype(F32)
    for k in range(1, half):
        acc += r2[1, k].astype(F32)
    for i in range(fold):
        for c in range(wide // LANES):
            gv_ref[:, i * (wide // LANES) + c] = acc[
                i * rows_pp : (i + 1) * rows_pp, c * LANES : (c + 1) * LANES
            ]
    gd_ref[...] = acc[:rows_pp, wide:]

    for m in range(members):
        swaps[m].wait_send()
        hands[m].wait_send()
        pl.when(has_onward)(passes[m].wait_send)
        pl.when(has_back)(crosses[m].wait_send)


def finish(channels, tot_in, sens_in, gv_in, gd_in, tot_ref, sens_ref, gv_ref, gd_ref):
    tot_ref[...] = tot_in[:1, :1]
    sens_ref[...] = sens_in[...]
    gv_ref[...] = gv_in[...]
    if gd_ref.shape[-1] != LANES:
        gd_ref[...] = gd_in[:, :channels]
        return
    for i in range(gd_ref.shape[0]):
        at, parts = i * LANES, []
        while at < (i + 1) * LANES:
            row, c = divmod(at, channels)
            n = min(channels - c, (i + 1) * LANES - at)
            parts.append(gd_in[row : row + 1, c : c + n])
            at += n
        gd_ref[i : i + 1] = jnp.concatenate(parts, axis=1)


def per_device(
    embeddings,
    reference_analysis,
    attention_matrix,
    readout_matrix,
    adjacent_blocks,
    companion_matrix,
    continent_indicator,
    zonal_strip,
):
    members, points, width = embeddings.shape
    channels = reference_analysis.shape[0]
    n_ens, n_grid = lax.axis_size("ens"), lax.axis_size("grid")
    ext = points + 2 * RIM
    pairs = width // LANES
    rows_pp = width // (n_ens * n_grid)
    fold = max(1, 16 // rows_pp)
    chunk = (rows_pp * fold, width // fold + LANES)
    n_far = n_ens // 2
    patches = points // SCORED_ENTRIES
    assert points == RIM and n_grid % 2 == 0 and members > 1
    vmem = pl.BlockSpec(memory_space=pltpu.VMEM)
    smem = pl.BlockSpec(memory_space=pltpu.SMEM)
    dma = pltpu.SemaphoreType.DMA
    V = pltpu.VMEM
    scratch = [
        V((width, 3 * width), BF16),
        V((LANES, width), BF16),
        V((points, LANES), F32),
        V((points, LANES), F32),
        V((members, ext, width), BF16),
        V((members, width, ext), BF16),
        V((members, points, width), BF16),
        V((members, ext, 2 * width), BF16),
        V((2 * points, ext), F32),
        V((members * pairs, 2 * points, ext), F32),
        V((members * pairs, ext, 2 * points), BF16),
        V((members, points, width), F32),
        V((members * points, width), BF16),
        V((width, members * points), BF16),
        V((members, points, width), BF16),
        V((members, points, width), BF16),
        V((members, ext, 2 * width), BF16),
        V((n_ens, members, points, LANES), F32),
        V((n_ens, n_grid) + chunk, BF16),
        V((n_far, n_grid) + chunk, BF16),
        V((max(1, n_far - 1), n_grid) + chunk, BF16),
        V((max(1, n_far - 1), n_grid) + chunk, BF16),
        V((2, n_grid // 2) + chunk, BF16),
        V((2, n_grid // 2) + chunk, BF16),
        V((members, 2, RIM, width), BF16),
        V((members, RIM, width), BF16),
        V((members, RIM, width), BF16),
        V((members, RIM, width), BF16),
        V((members * pairs, 2 * points, ext), BF16),
        V((n_ens, 8, LANES), F32),
        V((n_grid, 8, LANES), F32),
        dma(()),
        dma((2 * members,)), dma((2 * members,)),
        dma((members * n_ens,)), dma((members * n_ens,)),
        dma((n_far,)), dma((n_far,)),
        dma((n_far * 2,)), dma((n_far * 2,)),
        dma((n_grid,)), dma((n_grid,)),
        dma((2 * members,)), dma((2 * members,)),
        dma((n_ens,)), dma((n_ens,)),
        dma((n_grid,)), dma((n_grid,)),
    ]
    total, sens, grad_value, grad_dec = pl.pallas_call(
        functools.partial(kernel, n_ens, n_grid, channels),
        out_shape=(
            jax.ShapeDtypeStruct((8, LANES), F32),
            jax.ShapeDtypeStruct((members, points, width), F32),
            jax.ShapeDtypeStruct((rows_pp, width // LANES, LANES), F32),
            jax.ShapeDtypeStruct((rows_pp, LANES), F32),
        ),
        in_specs=[smem, smem, vmem, vmem, pl.BlockSpec(memory_space=pl.ANY), vmem, vmem, vmem],
        out_specs=(vmem,) * 4,
        scratch_shapes=scratch,
        compiler_params=pltpu.CompilerParams(
            collective_id=0, has_side_effects=True, vmem_limit_bytes=60 * 1024 * 1024
        ),
    )(
        adjacent_blocks,
        companion_matrix,
        embeddings,
        reference_analysis,
        attention_matrix,
        readout_matrix.T,
        continent_indicator.reshape(patches, SCORED_ENTRIES),
        zonal_strip.reshape(patches, SCORED_ENTRIES),
    )
    flat = rows_pp * channels
    dec_shape = (flat // LANES, LANES) if flat % LANES == 0 else (rows_pp, channels)
    total, sens, grad_value, grad_dec = pl.pallas_call(
        functools.partial(finish, channels),
        out_shape=(
            jax.ShapeDtypeStruct((1, 1), F32),
            jax.ShapeDtypeStruct(sens.shape, F32),
            jax.ShapeDtypeStruct(grad_value.shape, F32),
            jax.ShapeDtypeStruct(dec_shape, F32),
        ),
        in_specs=[vmem] * 4,
        out_specs=(vmem,) * 4,
        compiler_params=pltpu.CompilerParams(vmem_limit_bytes=60 * 1024 * 1024),
    )(total, sens, grad_value, grad_dec)
    return (
        total.reshape(()),
        sens,
        grad_value.reshape(-1),
        grad_dec.reshape(-1),
    )


def solution(mesh):
    in_specs = (
        P("ens", "grid", None),
        P(None, "grid"),
        P(),
        P(),
        P("grid", None),
        P(),
        P("grid"),
        P("grid"),
    )
    out_specs = (P(), P("ens", "grid", None), P(("ens", "grid")), P(("ens", "grid")))
    return jax.shard_map(
        per_device, mesh=mesh, in_specs=in_specs, out_specs=out_specs, check_vma=False
    )
```

```python
import functools
import math

import jax
import jax.numpy as jnp
from jax import lax
from jax.experimental import pallas as pl
from jax.experimental.pallas import tpu as pltpu
from jax.sharding import PartitionSpec as P

HEADS = 16
QB = 64
R_BLK = 2
NB = 3
SCORED_ENTRIES = 128
NLAT = 721
EPSILON = 1e-06
RIM = R_BLK * QB
LANES = 128
NEG = -1e30

F32 = jnp.float32
BF16 = jnp.bfloat16
MESH = pl.DeviceIdType.MESH


def mm(a, b):
    return lax.dot_general(a, b, (((1,), (0,)), ((), ())), preferred_element_type=F32)


def mm_nt(a, b):
    return lax.dot_general(a, b, (((1,), (1,)), ((), ())), preferred_element_type=F32)


def mm_tn(a, b):
    return lax.dot_general(a, b, (((0,), (0,)), ((), ())), preferred_element_type=F32)


def rms_scale(values):
    return lax.rsqrt(jnp.mean(values * values, axis=-1, keepdims=True) + EPSILON)


def kernel(
    n_ens, n_grid, channels,
    adj_ref, comp_ref, x_ref, ref_ref, w_hbm, r_ref, land_ref, strip_ref,
    tot_ref, out_ref, gv_ref, gd_ref,
    w_ref, rt, tgt, wgts, nrm, nrm_t, q_s, kv, lc_s, ac_s, ac_t, state, hid, hid_t, go, gq, gkv, fc,
    vp, rc0, s1, rc1, s2, r2, gnr, gx, hand, gnx, ds_s, tq, tg,
    w_sem, halo_send, halo_recv, fc_send, fc_recv, core_send, core_recv,
    x_send, x_recv, g_send, g_recv, back_send, back_recv,
    tq_send, tq_recv, tg_send, tg_recv,
):
    members, points, width = x_ref.shape
    ext = points + 2 * RIM
    nblk = points // QB
    pairs = width // LANES
    rounds = comp_ref.shape[0]
    patches = points // SCORED_ENTRIES
    rows_pp = width // (n_ens * n_grid)
    fold = max(1, 16 // rows_pp)
    wide = width // fold
    n_far = n_ens // 2
    half = n_grid // 2
    e = lax.axis_index("ens")
    g = lax.axis_index("grid")
    core = e % 2
    far = e // 2
    scale = 1.0 / math.sqrt(width // HEADS)

    def ens_copy(src, dst, ss, rs, to):
        return pltpu.make_async_remote_copy(
            src_ref=src, dst_ref=dst, send_sem=ss, recv_sem=rs,
            device_id={"ens": to}, device_id_type=MESH,
        )

    def grid_copy(src, dst, ss, rs, to):
        return pltpu.make_async_remote_copy(
            src_ref=src, dst_ref=dst, send_sem=ss, recv_sem=rs,
            device_id={"grid": to}, device_id_type=MESH,
        )

    w_copy = pltpu.make_async_copy(w_hbm, w_ref, w_sem)
    w_copy.start()
    barrier = pltpu.get_barrier_semaphore()
    for k in range(1, n_ens):
        pl.semaphore_signal(barrier, inc=1, device_id={"ens": (e + k) % n_ens}, device_id_type=MESH)
    for k in range(1, n_grid):
        pl.semaphore_signal(barrier, inc=1, device_id={"grid": (g + k) % n_grid}, device_id_type=MESH)

    @pl.when(g == 0)
    def _():
        nrm[:, :RIM] = jnp.zeros((members, RIM, width), BF16)

    @pl.when(g == n_grid - 1)
    def _():
        nrm[:, RIM + points :] = jnp.zeros((members, RIM, width), BF16)

    odd = g % 2
    far_row = RIM + points
    bit = RIM // 2

    def near(h):
        return pl.ds(pl.multiple_of((1 - odd) * far_row + h * bit, bit), bit)

    def away(h):
        return pl.ds(pl.multiple_of(odd * far_row + h * bit, bit), bit)

    mate = g + 1 - 2 * odd
    onward = g + 2 - 4 * odd
    back_to = g - 2 + 4 * odd
    has_onward = (onward >= 0) & (onward < n_grid)
    has_back = (back_to >= 0) & (back_to < n_grid)
    onward_id = (onward + n_grid) % n_grid
    back_id = (back_to + n_grid) % n_grid
    swaps, passes = [], []
    for m in range(members):
        lat = x_ref[m].astype(F32)
        nrm[m, RIM : RIM + points] = (lat * rms_scale(lat)).astype(BF16)
        if m == 0:
            pl.semaphore_wait(barrier, n_ens + n_grid - 2)
        for h in range(2):
            i = 2 * m + h
            j = 2 * members + i
            cp = grid_copy(nrm.at[m, pl.ds(RIM + h * bit, bit)], nrm.at[m, away(h)],
                           halo_send.at[i], halo_recv.at[i], mate)
            cp.start()
            swaps.append(cp)
            passes.append(grid_copy(nrm.at[m, near(h)], nrm.at[m, away(h)],
                                    halo_send.at[j], halo_recv.at[j], onward_id))

    def pass_on(m, h):
        swaps[2 * m + h].wait_recv()
        pl.when(has_onward)(passes[2 * m + h].start)

    out_ref[...] = jnp.zeros(out_ref.shape, F32)
    out_ref[0, :channels] = r_ref[...].astype(F32)
    out_ref[1, :channels, :points] = ref_ref[...]
    rt[...] = out_ref[0, :LANES].astype(BF16)
    for j in range(patches):
        rows = slice(j * SCORED_ENTRIES, (j + 1) * SCORED_ENTRIES)
        tgt[rows] = out_ref[1, :LANES, rows].T
        phase = (strip_ref[j : j + 1].astype(F32) + 0.5) * (math.pi / NLAT) - 0.5 * math.pi
        wrow = jnp.cos(phase) * (1.0 + land_ref[j : j + 1].astype(F32))
        wgts[rows] = jnp.broadcast_to(wrow, (LANES, SCORED_ENTRIES)).T

    col = lax.broadcasted_iota(jnp.int32, (1, ext), 1)
    for b in range(nblk):
        count = jnp.zeros((1, ext), F32)
        for n in range(NB):
            first = (adj_ref[b, n] - g * nblk + R_BLK) * QB
            count += jnp.where((col >= first) & (col < first + QB), 1.0, 0.0)
        rows = jnp.where(count > 0.0, jnp.log(jnp.maximum(count, 1.0)), NEG)
        rows = jnp.broadcast_to(rows, (QB, ext))
        lc_s[b * QB : (b + 1) * QB] = rows
        lc_s[points + b * QB : points + (b + 1) * QB] = rows

    w_copy.wait()
    tile = 512

    @pl.loop(0, width // tile)
    def _(t):
        own = nrm[:, RIM : RIM + points].reshape(members * points, width)
        c = pl.multiple_of(t * tile, tile)
        res = mm(own, w_ref[:, pl.ds(c, tile)]).astype(BF16) * scale
        q_s[:, :, pl.ds(c, tile)] = res.astype(BF16).reshape(members, points, tile)

    pass_on(0, 0)
    pass_on(0, 1)

    @pl.loop(0, 2 * width // tile)
    def _(t):
        own = nrm[:, RIM : RIM + points].reshape(members * points, width)
        c = pl.multiple_of(t * tile, tile)
        wt = w_ref[:, pl.ds(pl.multiple_of(c + width, tile), tile)]
        kv[:, RIM : RIM + points, pl.ds(c, tile)] = mm(own, wt).astype(BF16).reshape(
            members, points, tile
        )

    head_a = lax.broadcasted_iota(jnp.int32, (points, LANES), 1) < LANES // 2

    def stacked(v):
        zero = jnp.zeros_like(v)
        return jnp.concatenate([jnp.where(head_a, v, zero), jnp.where(head_a, zero, v)], axis=0)

    def merged(v):
        return jnp.where(head_a, v[:points], v[points:])

    group = 2

    def cols(c):
        c = pl.multiple_of(c * LANES, LANES)
        return pl.ds(c, LANES), pl.ds(pl.multiple_of(c + width, LANES), LANES)

    sends = []
    for m in range(members):
        if m + 1 < members:
            pass_on(m + 1, 0)
        for h in range(2):
            pl.when(has_back)(passes[2 * m + h].wait_recv)

        @pl.loop(0, 2 * width // tile)
        def _(t):
            c = pl.multiple_of(t * tile, tile)
            wt = w_ref[:, pl.ds(pl.multiple_of(c + width, tile), tile)]
            rim = jnp.concatenate([nrm[m, :RIM], nrm[m, RIM + points :]], axis=0)
            res = mm(rim, wt).astype(BF16)
            kv[m, :RIM, pl.ds(c, tile)] = res[:RIM]
            kv[m, RIM + points :, pl.ds(c, tile)] = res[RIM:]

        if m + 1 < members:
            pass_on(m + 1, 1)

        @pl.loop(0, pairs // group)
        def _(it):
            log_count = lc_s[...]
            at = [cols(it * group + i) for i in range(group)]
            ss = [mm_nt(stacked(q_s[m, :, ck]), kv[m, :, ck]) for ck, _ in at]
            ss = [s + log_count for s in ss]
            ex = [jnp.exp(s - jnp.max(s, axis=-1, keepdims=True)) for s in ss]
            aa = [x * (1.0 / jnp.sum(x, axis=-1, keepdims=True)) for x in ex]
            res = [merged(mm(a.astype(BF16), kv[m, :, cv])) for a, (_, cv) in zip(aa, at)]
            for i in range(group):
                ac_s[m * pairs + it * group + i] = aa[i]
                state[m, :, at[i][0]] = res[i]

        st = x_ref[m].astype(F32) + state[m]
        state[m] = st
        h = (st * rms_scale(st)).astype(BF16)
        hid[m * points : (m + 1) * points] = h
        fc[e, m] = mm_nt(h, rt[...])
        for k in range(1, n_ens):
            i = m * n_ens + k
            cp = ens_copy(fc.at[e, m], fc.at[e, m], fc_send.at[i], fc_recv.at[i], (e + k) % n_ens)
            cp.start()
            sends.append(cp)

    @pl.loop(0, members * pairs)
    def _(it):
        ac_t[it] = ac_s[it].astype(BF16).T

    for m in range(members):
        nrm_t[m] = nrm[m].T
    hid_t[...] = hid[...].T

    for cp in sends:
        cp.wait()

    lane = lax.broadcasted_iota(jnp.int32, (1, LANES), 1)
    valid = lane < channels
    total = jnp.zeros((1, LANES), F32)
    g16 = []
    for m in range(members):
        parts = []
        for j in range(patches):
            rows = slice(j * SCORED_ENTRIES, (j + 1) * SCORED_ENTRIES)
            rnd = (lane + g * patches + j) % rounds
            partner = jnp.zeros((1, LANES), jnp.int32)
            for r in range(rounds):
                partner = jnp.where(rnd == r, comp_ref[r, e * members + m], partner)
            f = fc[e, m, rows]
            pf = jnp.zeros_like(f)
            for n in range(n_ens * members):
                pf = jnp.where(partner == n, fc[n // members, n % members, rows], pf)
            wgt = wgts[rows]
            err = f - tgt[rows]
            dif = f - pf
            dt = jnp.sqrt(jnp.sum(wgt * err * err, axis=0, keepdims=True) + EPSILON)
            dp = jnp.sqrt(jnp.sum(wgt * dif * dif, axis=0, keepdims=True) + EPSILON)
            total += jnp.where(valid, dt - 0.5 * dp, 0.0)
            parts.append((wgt * err / dt - wgt * dif / dp).astype(BF16))
        g16.append(jnp.concatenate(parts, axis=0) if patches > 1 else parts[0])
    g_all = jnp.concatenate(g16, axis=0)

    tq[e] = jnp.broadcast_to(jnp.sum(total, axis=-1, keepdims=True), (8, LANES))
    tqs = []
    for k in range(1, n_ens):
        cp = ens_copy(tq.at[e], tq.at[e], tq_send.at[k], tq_recv.at[k], (e + k) % n_ens)
        cp.start()
        tqs.append(cp)

    for m in range(members):
        gh = mm(g16[m], rt[...])
        st = state[m]
        inv = rms_scale(st)
        y = st * inv
        gs = inv * (gh - y * jnp.mean(gh * y, axis=-1, keepdims=True))
        out_ref[m] = gs
        go[m] = gs.astype(BF16)

    for m in range(members):
        @pl.loop(0, pairs // group)
        def _(it):
            at = [cols(it * group + i) for i in range(group)]
            res = [mm(ac_t[m * pairs + it * group + i], stacked(go[m, :, at[i][0]])).astype(BF16)
                   for i in range(group)]
            for i in range(group):
                gkv[m, :, at[i][1]] = res[i]

    per_ens = width // n_ens

    def folded(v, count):
        v = v.reshape(n_grid, rows_pp, count)
        v = jnp.stack([v[i] for i in list(range(0, n_grid, 2)) + list(range(1, n_grid, 2))])
        if fold > 1:
            step = count // fold
            v = jnp.concatenate([v[:, :, i * step : (i + 1) * step] for i in range(fold)], axis=1)
        return v.astype(BF16)

    @pl.loop(0, n_ens)
    def _(qd):
        d = pl.ds(pl.multiple_of(qd * per_ens, per_ens), per_ens)
        acc = mm(nrm_t[0, d], gkv[0, :, width:])
        for m in range(1, members):
            acc += mm(nrm_t[m, d], gkv[m, :, width:])
        vp[qd, :, :, :wide] = folded(acc, width)
        dec = mm(hid_t[d], g_all)
        if fold > 1:
            dec = jnp.concatenate(
                [dec, jnp.zeros((per_ens, LANES * (fold - 1)), F32)], axis=1
            )
        vp[qd, :, :, wide:] = folded(dec, LANES * fold)

    cores = []
    for k in range(n_far):
        f = (far + 1 + k) % n_far
        cp = ens_copy(vp.at[2 * f + 1 - core], rc0.at[f], core_send.at[k], core_recv.at[k],
                      2 * far + 1 - core)
        cp.start()
        cores.append(cp)

    for cp in tqs:
        cp.wait()
    tg[g] = functools.reduce(lambda a, b: a + b, [tq[i] for i in range(n_ens)])
    tgs = []
    for k in range(1, n_grid):
        cp = grid_copy(tg.at[g], tg.at[g], tg_send.at[k], tg_recv.at[k], (g + k) % n_grid)
        cp.start()
        tgs.append(cp)

    def back(m, start, stop):
        @pl.loop(start, stop)
        def _(it):
            at = [cols(it * group + i) for i in range(group)]
            aa = [ac_s[m * pairs + it * group + i] for i in range(group)]
            da = [mm_nt(stacked(go[m, :, ck]), kv[m, :, cv]) for ck, cv in at]
            ds = [a * (d - jnp.sum(a * d, axis=-1, keepdims=True)) for a, d in zip(aa, da)]
            ds = [d.astype(BF16) for d in ds]
            dk = [mm_tn(d, stacked(q_s[m, :, ck])).astype(BF16) for d, (ck, _) in zip(ds, at)]
            for i in range(group):
                ds_s[m * pairs + it * group + i] = ds[i]
                gkv[m, :, at[i][0]] = dk[i]

    def back_query(m):
        @pl.loop(0, pairs // group)
        def _(it):
            at = [cols(it * group + i) for i in range(group)]
            dq = [merged(mm(ds_s[m * pairs + it * group + i], kv[m, :, at[i][0]])) * scale
                  for i in range(group)]
            for i in range(group):
                gq[m, :, at[i][0]] = dq[i].astype(BF16)

    dt_tile = 256

    crosses, hands = [], []
    for i in range(2 * members):
        m, sl, j = i // 2, pl.ds((i % 2) * bit, bit), 2 * members + i
        crosses.append(grid_copy(gnr.at[m, odd, sl], gx.at[m, sl],
                                 back_send.at[i], back_recv.at[i], back_id))
        hands.append(grid_copy(hand.at[m, sl], gnx.at[m, sl],
                               back_send.at[j], back_recv.at[j], mate))

    def rim_back(m):
        @pl.loop(0, width // dt_tile)
        def _(t):
            d = pl.ds(pl.multiple_of(t * dt_tile, dt_tile), dt_tile)
            rim = jnp.concatenate([gkv[m, :RIM], gkv[m, RIM + points :]], axis=0)
            res = mm_nt(rim, w_ref[d, width:]).astype(BF16)
            gnr[m, :, :, d] = res.reshape(2, RIM, dt_tile)

        for h in range(2):
            pl.when(has_back)(crosses[2 * m + h].start)

    def hand_over(m, h):
        sl = pl.ds(h * bit, bit)
        hand[m, sl] = gnr[m, 1 - odd, sl]

        @pl.when(has_onward)
        def _():
            crosses[2 * m + h].wait_recv()
            hand[m, sl] = (gnr[m, 1 - odd, sl].astype(F32) + gx[m, sl].astype(F32)).astype(BF16)

        hands[2 * m + h].start()

    xs = []

    def part_of(c):
        return pl.ds(((1 - odd) if c == 0 else odd) * half, half)

    def far_stage():
        for k in range(n_far - 1):
            cores[k].wait()
            f = (far + 1 + k) % n_far
            for c in range(2):
                sl = part_of(c)
                s1[k, sl] = (vp[2 * f + core, sl].astype(F32) + rc0[f, sl].astype(F32)).astype(BF16)
                cp = ens_copy(s1.at[k, sl], rc1.at[k, sl], x_send.at[k * 2 + c],
                              x_recv.at[k * 2 + c], 2 * f + core)
                cp.start()
                xs.append(cp)
        cores[n_far - 1].wait()

    def part_sum(c):
        sl = part_of(c)
        part = vp[2 * far + core, sl].astype(F32) + rc0[far, sl].astype(F32)
        for k in range(n_far - 1):
            xs[k * 2 + c].wait()
            part += rc1[k, sl].astype(F32)
        return part

    mate_copy = grid_copy(s2.at[0], r2.at[0], g_send.at[0], g_recv.at[0], mate)
    place = g // 2
    gcs = [
        grid_copy(s2.at[1, (place + k) % half], r2.at[1, k], g_send.at[k], g_recv.at[k],
                  2 * ((place + k) % half) + odd)
        for k in range(1, half)
    ]

    def mate_stage():
        s2[0] = part_sum(0).astype(BF16)
        mate_copy.start()

    def grid_stage():
        part = part_sum(1)
        mate_copy.wait()
        s2[1] = (part + r2[0].astype(F32)).astype(BF16)
        for cp in gcs:
            cp.start()

    steps = pairs // group
    for m in range(members):
        if m == 0:
            back(m, 0, 1)
            far_stage()
            back(m, 1, steps - 1)
            mate_stage()
            back(m, steps - 1, steps)
        elif m == 1:
            back(m, 0, 1)
            grid_stage()
            back(m, 1, 2)
            hand_over(0, 0)
            hand_over(0, 1)
            back(m, 2, steps)
        else:
            back(m, 0, steps)
        rim_back(m)

    for m in range(members):
        back_query(m)
        for late in range(1, members):
            if m < 2:
                hand_over(late, m)

    @pl.loop(0, width // dt_tile)
    def _(t):
        d = pl.ds(pl.multiple_of(t * dt_tile, dt_tile), dt_tile)
        res = mm_nt(gq[...].reshape(members * points, width), w_ref[d, :width])
        res += mm_nt(gkv[:, RIM : RIM + points].reshape(members * points, 2 * width),
                     w_ref[d, width:])
        state[:, :, d] = res.reshape(members, points, dt_tile)

    for cp in tgs:
        cp.wait()
    whole = functools.reduce(lambda a, b: a + b, [tg[i] for i in range(n_grid)])
    count = n_ens * members * channels * patches * n_grid
    tot_ref[...] = whole * (1.0 / count)

    for m in range(members):
        for h in range(2):
            hands[2 * m + h].wait_recv()
        lat = x_ref[m].astype(F32)
        inv = rms_scale(lat)
        y = lat * inv
        gn = state[m] + gnx[m].astype(F32)
        out_ref[m] += inv * (gn - y * jnp.mean(gn * y, axis=-1, keepdims=True))

    for cp in gcs:
        cp.wait()
    acc = s2[1, place].astype(F32)
    for k in range(1, half):
        acc += r2[1, k].astype(F32)
    for i in range(fold):
        for c in range(wide // LANES):
            gv_ref[:, i * (wide // LANES) + c] = acc[
                i * rows_pp : (i + 1) * rows_pp, c * LANES : (c + 1) * LANES
            ]
    gd_ref[...] = acc[:rows_pp, wide:]

    for i in range(2 * members):
        swaps[i].wait_send()
        hands[i].wait_send()
        pl.when(has_onward)(passes[i].wait_send)
        pl.when(has_back)(crosses[i].wait_send)


def finish(channels, tot_in, sens_in, gv_in, gd_in, tot_ref, sens_ref, gv_ref, gd_ref):
    tot_ref[...] = tot_in[:1, :1]
    sens_ref[...] = sens_in[...]
    gv_ref[...] = gv_in[...]
    if gd_ref.shape[-1] != LANES:
        gd_ref[...] = gd_in[:, :channels]
        return
    for i in range(gd_ref.shape[0]):
        at, parts = i * LANES, []
        while at < (i + 1) * LANES:
            row, c = divmod(at, channels)
            n = min(channels - c, (i + 1) * LANES - at)
            parts.append(gd_in[row : row + 1, c : c + n])
            at += n
        gd_ref[i : i + 1] = jnp.concatenate(parts, axis=1)


def per_device(
    embeddings,
    reference_analysis,
    attention_matrix,
    readout_matrix,
    adjacent_blocks,
    companion_matrix,
    continent_indicator,
    zonal_strip,
):
    members, points, width = embeddings.shape
    channels = reference_analysis.shape[0]
    n_ens, n_grid = lax.axis_size("ens"), lax.axis_size("grid")
    ext = points + 2 * RIM
    pairs = width // LANES
    rows_pp = width // (n_ens * n_grid)
    fold = max(1, 16 // rows_pp)
    chunk = (rows_pp * fold, width // fold + LANES)
    n_far = n_ens // 2
    patches = points // SCORED_ENTRIES
    assert points == RIM and n_grid % 2 == 0 and members > 1
    vmem = pl.BlockSpec(memory_space=pltpu.VMEM)
    smem = pl.BlockSpec(memory_space=pltpu.SMEM)
    dma = pltpu.SemaphoreType.DMA
    V = pltpu.VMEM
    scratch = [
        V((width, 3 * width), BF16),
        V((LANES, width), BF16),
        V((points, LANES), F32),
        V((points, LANES), F32),
        V((members, ext, width), BF16),
        V((members, width, ext), BF16),
        V((members, points, width), BF16),
        V((members, ext, 2 * width), BF16),
        V((2 * points, ext), F32),
        V((members * pairs, 2 * points, ext), F32),
        V((members * pairs, ext, 2 * points), BF16),
        V((members, points, width), F32),
        V((members * points, width), BF16),
        V((width, members * points), BF16),
        V((members, points, width), BF16),
        V((members, points, width), BF16),
        V((members, ext, 2 * width), BF16),
        V((n_ens, members, points, LANES), F32),
        V((n_ens, n_grid) + chunk, BF16),
        V((n_far, n_grid) + chunk, BF16),
        V((max(1, n_far - 1), n_grid) + chunk, BF16),
        V((max(1, n_far - 1), n_grid) + chunk, BF16),
        V((2, n_grid // 2) + chunk, BF16),
        V((2, n_grid // 2) + chunk, BF16),
        V((members, 2, RIM, width), BF16),
        V((members, RIM, width), BF16),
        V((members, RIM, width), BF16),
        V((members, RIM, width), BF16),
        V((members * pairs, 2 * points, ext), BF16),
        V((n_ens, 8, LANES), F32),
        V((n_grid, 8, LANES), F32),
        dma(()),
        dma((4 * members,)), dma((4 * members,)),
        dma((members * n_ens,)), dma((members * n_ens,)),
        dma((n_far,)), dma((n_far,)),
        dma((n_far * 2,)), dma((n_far * 2,)),
        dma((n_grid,)), dma((n_grid,)),
        dma((4 * members,)), dma((4 * members,)),
        dma((n_ens,)), dma((n_ens,)),
        dma((n_grid,)), dma((n_grid,)),
    ]
    total, sens, grad_value, grad_dec = pl.pallas_call(
        functools.partial(kernel, n_ens, n_grid, channels),
        out_shape=(
            jax.ShapeDtypeStruct((8, LANES), F32),
            jax.ShapeDtypeStruct((members, points, width), F32),
            jax.ShapeDtypeStruct((rows_pp, width // LANES, LANES), F32),
            jax.ShapeDtypeStruct((rows_pp, LANES), F32),
        ),
        in_specs=[smem, smem, vmem, vmem, pl.BlockSpec(memory_space=pl.ANY), vmem, vmem, vmem],
        out_specs=(vmem,) * 4,
        scratch_shapes=scratch,
        compiler_params=pltpu.CompilerParams(
            collective_id=0, has_side_effects=True, vmem_limit_bytes=60 * 1024 * 1024
        ),
    )(
        adjacent_blocks,
        companion_matrix,
        embeddings,
        reference_analysis,
        attention_matrix,
        readout_matrix.T,
        continent_indicator.reshape(patches, SCORED_ENTRIES),
        zonal_strip.reshape(patches, SCORED_ENTRIES),
    )
    flat = rows_pp * channels
    dec_shape = (flat // LANES, LANES) if flat % LANES == 0 else (rows_pp, channels)
    total, sens, grad_value, grad_dec = pl.pallas_call(
        functools.partial(finish, channels),
        out_shape=(
            jax.ShapeDtypeStruct((1, 1), F32),
            jax.ShapeDtypeStruct(sens.shape, F32),
            jax.ShapeDtypeStruct(grad_value.shape, F32),
            jax.ShapeDtypeStruct(dec_shape, F32),
        ),
        in_specs=[vmem] * 4,
        out_specs=(vmem,) * 4,
        compiler_params=pltpu.CompilerParams(vmem_limit_bytes=60 * 1024 * 1024),
    )(total, sens, grad_value, grad_dec)
    return (
        total.reshape(()),
        sens,
        grad_value.reshape(-1),
        grad_dec.reshape(-1),
    )


def solution(mesh):
    in_specs = (
        P("ens", "grid", None),
        P(None, "grid"),
        P(),
        P(),
        P("grid", None),
        P(),
        P("grid"),
        P("grid"),
    )
    out_specs = (P(), P("ens", "grid", None), P(("ens", "grid")), P(("ens", "grid")))
    return jax.shard_map(
        per_device, mesh=mesh, in_specs=in_specs, out_specs=out_specs, check_vma=False
    )
```
